256 devices in a mesh: tm: 8 (over z_lo, core), height: 8 (over z_hi, y), head: 4 (over x).
Axes of the slice: x: 4, y: 4, z: 8 (z_hi: 2, z_lo: 4; z = z_hi * 4 + z_lo), core: 2. Of those that a mesh axis runs over, the one named last changes fastest.
Arguments:
- latents: bfloat16 [16, 64, 16, 1152], P('tm', 'height', None, 'head'), may hold values from -45 to 45
- modulation: float32 [9, 1152], replicated, may hold values from -3 to 3
- spatial_qkv: bfloat16 [3, 1152, 1152], P(None, None, 'head'), may hold values from -2.563262 to 2.563262
- spatial_out: bfloat16 [1152, 1152], P('head'), may hold values from -1.5 to 1.5
- temporal_qkv: bfloat16 [3, 1152, 1152], P(None, None, 'head'), may hold values from -2.563262 to 2.563262
- temporal_out: bfloat16 [1152, 1152], P('head'), may hold values from -0.375 to 0.375
- mlp_up: bfloat16 [1152, 4608], P(None, 'head'), may hold values from -0.1875 to 0.1875
- mlp_down: bfloat16 [4608, 1152], P('head'), may hold values from -0.09375 to 0.09375
Outputs:
- result: bfloat16 [16, 64, 16, 1152], P('tm', 'height', None, 'head')
The draws below stay inside these ranges and needn't reach their ends.
All inputs are finite; a program needn't handle non-finite values.
Results may differ from the reference program's by a relative error of at most 0.04.
Values may be sent and summed in bfloat16 or wider, within the bound.
A program may use at most 128 MiB of HBM per device.

```python
import math
import jax
import jax.numpy as jnp
from jax import lax

D = 1152
HEAD_DIM = 72
FF = 4608
TILE = 8
COLS = 16
FRAMES = 16
ROWS = 64
N_HEAD = 4


def normal_weights(key):
    base = jnp.clip(jax.random.normal(key, (3, D, D), jnp.float32), -4.0, 4.0)
    return (base / math.sqrt(D)).astype(jnp.bfloat16)


def draw_latents(key, part):
    key = jax.random.fold_in(key, 7)
    first_key, second_key, third_key = jax.random.split(key, 3)
    shape_all = (FRAMES, ROWS, COLS, D)
    column_scale = jnp.exp(jax.random.uniform(first_key, (D,), jnp.float32, math.log(0.3), math.log(3.0)))
    row_scale = jnp.exp(jax.random.uniform(second_key, (FRAMES, ROWS, COLS, 1), jnp.float32, math.log(0.3), math.log(3.0)))
    base = jnp.clip(jax.random.normal(third_key, shape_all, jnp.float32), -5.0, 5.0)
    return (base * column_scale * row_scale).astype(jnp.float32).astype(jnp.bfloat16)


def draw_modulation(key, part):
    key = jax.random.fold_in(key, 17)
    first_key, second_key, third_key = jax.random.split(key, 3)
    base = jnp.clip(0.5 * jax.random.normal(first_key, (9, D), jnp.float32), -3.0, 3.0)
    magnitude = jax.random.uniform(second_key, (2, D), jnp.float32, 1.5, 3.0)
    signs = jnp.where(jax.random.uniform(third_key, (2, D), jnp.float32) < 0.5, -1.0, 1.0)
    gates = magnitude * signs
    base = base.at[5].set(gates[0])
    base = base.at[8].set(gates[1])
    return base


def draw_spatial_qkv(key, part):
    key = jax.random.fold_in(key, 11)
    return normal_weights(key)


def draw_temporal_qkv(key, part):
    key = jax.random.fold_in(key, 13)
    return normal_weights(key)


def level_of(rng, extent, cuts, least, largest):
    gain, own = 1.0, jax.random.fold_in(rng, 6)
    for position, blocks in cuts:
        steps = jnp.exp(jax.random.uniform(jax.random.fold_in(own, position), (blocks,), jnp.float32, least / len(cuts), largest / len(cuts)))
        gain = gain * jnp.repeat(steps, extent[position] // blocks).reshape([-1 if axis == position else 1 for axis in range(len(extent))])
    return gain


def bell_draw(own_key, dims, deviation, most, shards=(), kind=jnp.bfloat16):
    level = level_of(own_key, dims, shards, -0.22, 0.18) if shards else 1.0
    values = jax.random.normal(own_key, dims, jnp.float32) * deviation * level
    return jnp.minimum(jnp.maximum(values, -most), most).astype(kind)


def setup_inputs(seed: int = 0) -> dict:
    keys = jax.random.split(jax.random.key(seed), 9)
    return {
        "latents": draw_latents(jax.random.fold_in(keys[8], 71), 0),
        "modulation": draw_modulation(jax.random.fold_in(keys[8], 71), 0),
        "spatial_qkv": draw_spatial_qkv(jax.random.fold_in(keys[8], 71), 0),
        "spatial_out": bell_draw(keys[3], (D, D), (D // 64) ** -0.5, 1.5, ((0, 4),)),
        "temporal_qkv": draw_temporal_qkv(jax.random.fold_in(keys[8], 71), 0),
        "temporal_out": bell_draw(keys[5], (D, D), (D // 4) ** -0.5, 0.375, ((0, 4),)),
        "mlp_up": bell_draw(keys[6], (D, FF), D ** -0.5, 0.1875, ((1, 4),)),
        "mlp_down": bell_draw(keys[7], (FF, D), FF ** -0.5, 0.09375, ((0, 4),)),
    }


EPSILON = 1e-06

def modulate(values, shift_row, scale_row):
    data = values.astype(jnp.float32)
    mean_value = lax.optimization_barrier(jnp.mean(data, axis=-1, keepdims=True))
    centred = data - mean_value
    variance = lax.optimization_barrier(jnp.mean(centred * centred, axis=-1, keepdims=True))
    return (centred * lax.rsqrt(variance + EPSILON) * (1.0 + scale_row) + shift_row).astype(jnp.bfloat16)

def softmax_rows(scores):
    top_score = lax.optimization_barrier(jnp.max(scores, axis=-1, keepdims=True))
    expo = jnp.exp(scores - top_score)
    return expo / lax.optimization_barrier(jnp.sum(expo, axis=-1, keepdims=True))

def tile_form(tensor, tile_rows, tile_cols):
    frames_here = tensor.shape[0]
    width = tensor.shape[-1]
    shaped = tensor.reshape(frames_here, tile_rows, TILE, tile_cols, TILE, width)
    return shaped.transpose(0, 1, 3, 2, 4, 5).reshape(frames_here, tile_rows, tile_cols, TILE * TILE, width)

def grid_form(tensor, tile_rows, tile_cols):
    frames_here = tensor.shape[0]
    width = tensor.shape[-1]
    shaped = tensor.reshape(frames_here, tile_rows, tile_cols, TILE, TILE, width)
    return shaped.transpose(0, 1, 3, 2, 4, 5).reshape(frames_here, tile_rows * TILE, tile_cols * TILE, width)

def neighbourhood(padded, tile_rows, tile_cols):
    grid_tiles = tile_form(padded, tile_rows + 2, tile_cols + 2)
    pieces = [grid_tiles[:, row_step:row_step + tile_rows, col_step:col_step + tile_cols] for row_step in range(3) for col_step in range(3)]
    stacked = jnp.stack(pieces, axis=3)
    return stacked.reshape(padded.shape[0], tile_rows, tile_cols, 9 * TILE * TILE, padded.shape[-1])

def tile_mask(tile_rows, tile_cols, row_base, total_rows):
    order = jnp.arange(9)
    row_step = order // 3 - 1
    col_step = order % 3 - 1
    rows_at = row_base + jnp.arange(tile_rows)[:, None, None] + row_step[None, None, :]
    cols_at = jnp.arange(tile_cols)[None, :, None] + col_step[None, None, :]
    valid = (rows_at >= 0) & (rows_at < total_rows) & (cols_at >= 0) & (cols_at < tile_cols)
    return jnp.repeat(valid, TILE * TILE, axis=2)

def spatial_attend(queries, key_field, value_field, row_base, total_rows):
    frames_here, rows_here, cols_here, width = queries.shape
    heads_here = width // HEAD_DIM
    tile_rows = rows_here // TILE
    tile_cols = cols_here // TILE
    query_tiles = tile_form(queries, tile_rows, tile_cols).reshape(frames_here, tile_rows, tile_cols, TILE * TILE, heads_here, HEAD_DIM)
    padding = ((0, 0), (0, 0), (TILE, TILE), (0, 0))
    key_tiles = neighbourhood(jnp.pad(key_field, padding), tile_rows, tile_cols).reshape(frames_here, tile_rows, tile_cols, 9 * TILE * TILE, heads_here, HEAD_DIM)
    value_tiles = neighbourhood(jnp.pad(value_field, padding), tile_rows, tile_cols).reshape(frames_here, tile_rows, tile_cols, 9 * TILE * TILE, heads_here, HEAD_DIM)
    scores = jnp.einsum('fabqhd,fabkhd->fabhqk', query_tiles.astype(jnp.float32), key_tiles.astype(jnp.float32)) * HEAD_DIM ** (-0.5)
    valid = tile_mask(tile_rows, tile_cols, row_base, total_rows)[None, :, :, None, None, :]
    scores = jnp.where(valid, scores, -1e+30)
    weights = softmax_rows(scores).astype(jnp.bfloat16)
    mixed = jnp.einsum('fabhqk,fabkhd->fabqhd', weights.astype(jnp.float32), value_tiles.astype(jnp.float32)).astype(jnp.bfloat16)
    mixed = mixed.reshape(frames_here, tile_rows, tile_cols, TILE * TILE, width)
    return grid_form(mixed, tile_rows, tile_cols)

def temporal_attend(queries, key_field, value_field):
    frames_all, tokens_here, width = queries.shape
    heads_here = width // HEAD_DIM
    shape_heads = (frames_all, tokens_here, heads_here, HEAD_DIM)
    scores = jnp.einsum('qthd,kthd->thqk', queries.reshape(shape_heads).astype(jnp.float32), key_field.reshape(shape_heads).astype(jnp.float32)) * HEAD_DIM ** (-0.5)
    weights = softmax_rows(scores).astype(jnp.bfloat16)
    mixed = jnp.einsum('thqk,kthd->qthd', weights.astype(jnp.float32), value_field.reshape(shape_heads).astype(jnp.float32))
    return mixed.astype(jnp.bfloat16).reshape(frames_all, tokens_here, width)

def grouped(rows_in, weight):
    group_width = rows_in.shape[1] // N_HEAD
    total = jnp.zeros((rows_in.shape[0], weight.shape[1]), jnp.float32)
    for group in range(N_HEAD):
        term = jnp.dot(rows_in[:, group * group_width:(group + 1) * group_width], weight[group * group_width:(group + 1) * group_width], preferred_element_type=jnp.float32).astype(jnp.bfloat16)
        term = lax.optimization_barrier(term)
        total = total + term.astype(jnp.float32)
    return total

def reference(latents, modulation, spatial_qkv, spatial_out, temporal_qkv, temporal_out, mlp_up, mlp_down):
    tile_rows = ROWS // TILE

    def spatial_frame(frame):
        block = frame[None]
        normed = modulate(block, modulation[0], modulation[1])
        projected = jnp.einsum('frcd,sde->sfrce', normed.astype(jnp.float32), spatial_qkv.astype(jnp.float32)).astype(jnp.bfloat16)
        padded = jnp.pad(projected[1:], ((0, 0), (0, 0), (TILE, TILE), (0, 0), (0, 0)))
        attended = spatial_attend(projected[0], padded[0], padded[1], 0, tile_rows)
        summed = grouped(attended.reshape(-1, D), spatial_out).reshape(block.shape)
        return (block.astype(jnp.float32) + modulation[2] * summed).astype(jnp.bfloat16)[0]
    first = lax.map(spatial_frame, latents)

    def temporal_row(row_block):
        normed = modulate(row_block, modulation[3], modulation[4])
        projected = jnp.einsum('fcd,sde->sfce', normed.astype(jnp.float32), temporal_qkv.astype(jnp.float32)).astype(jnp.bfloat16)
        mixed = temporal_attend(projected[0], projected[1], projected[2])
        summed = grouped(mixed.reshape(-1, D), temporal_out).reshape(row_block.shape)
        second = (row_block.astype(jnp.float32) + modulation[5] * summed).astype(jnp.bfloat16)
        normed = modulate(second, modulation[6], modulation[7])
        hidden = jax.nn.gelu(jnp.dot(normed.reshape(-1, D), mlp_up, preferred_element_type=jnp.float32), approximate=True).astype(jnp.bfloat16)
        summed = grouped(hidden, mlp_down).reshape(row_block.shape)
        return (second.astype(jnp.float32) + modulation[8] * summed).astype(jnp.bfloat16)
    outcome = lax.map(temporal_row, first.transpose(1, 0, 2, 3))
    return outcome.transpose(1, 0, 2, 3)
```

```python
import functools

import jax
import jax.numpy as jnp
from jax import lax
from jax.experimental import pallas as pl
from jax.experimental.pallas import tpu as pltpu
from jax.sharding import PartitionSpec as P

D = 1152
HEAD_DIM = 72
PART = 288
COVER = 384
HEADS = 4
EPSILON = 1e-06
SCALE = HEAD_DIM ** (-0.5)
MESH = pl.DeviceIdType.MESH
F32 = jnp.float32
BF16 = jnp.bfloat16


def dot(a, b):
    return jnp.dot(a, b, preferred_element_type=F32)


def dot_t(a, b):
    return lax.dot_general(a, b, (((1,), (1,)), ((), ())), preferred_element_type=F32)


def modulate(v, shift, scale):
    mean = jnp.mean(v, axis=-1, keepdims=True)
    cen = v - mean
    var = jnp.mean(cen * cen, axis=-1, keepdims=True)
    return (cen * lax.rsqrt(var + EPSILON) * (1.0 + scale) + shift).astype(BF16)


def one_hot(rows, cols, source):
    r = lax.broadcasted_iota(jnp.int32, (rows, cols), 0)
    s = lax.broadcasted_iota(jnp.int32, (rows, cols), 1)
    return jnp.where(source(r) == s, 1.0, 0.0).astype(BF16)


def head_masks():
    lane = lax.broadcasted_iota(jnp.int32, (1, PART), 1)
    return [
        jnp.where((lane >= HEAD_DIM * h) & (lane < HEAD_DIM * (h + 1)), 1.0, 0.0).astype(F32)
        for h in range(HEADS)
    ]


def stack_heads(q, masks):
    q = q.astype(F32)
    return jnp.concatenate([(q * m).astype(BF16) for m in masks], axis=0)


def pick_heads(o, masks):
    n = o.shape[0] // HEADS
    total = o[0:n] * masks[0]
    for h in range(1, HEADS):
        total = total + o[h * n : (h + 1) * n] * masks[h]
    return total.astype(BF16)


def softmax(s):
    top = jnp.max(s, axis=-1, keepdims=True)
    e = jnp.exp(s - top)
    return (e / jnp.sum(e, axis=-1, keepdims=True)).astype(BF16)


def kernel(
    lat, mod, wqkv_h, wo_h, tqkv_h, to_h, up_h, dn_h, o_ref,
    w_s, w_so, w_t, w_to, w_up, w_dn,
    g, lfull, nrm, qb, kvo, inn, outr, ps, r4, lsel, fst, pk, a2, blk, att, pt, r7, blk2, hid, pm, r8, fin,
    wsem, s1, d1, sh, dh, s4, d4, s5, d5, s6, d6, s7, d7, s7b, d7b, s8, d8, s9, d9,
):
    tm = lax.axis_index("tm")
    he = lax.axis_index("height")
    x = lax.axis_index("head")
    zlo, c = tm // 2, tm % 2
    zhi, y = he // 4, he % 4
    d = (y + 4 - 2 * c) % 4
    w = d // 2
    t_me = ((d + 1) // 2) % 2
    m_me = 8 * t_me + 4 * w + zlo
    f_me = 4 * zlo + y
    at_home = y // 2 == c
    cross = zhi != c

    def dev(zlo, c, zhi, y, x):
        return (zlo * 2 + c, zhi * 4 + y, x)

    def xdev(k):
        return (tm, he, (x + k) % 4)

    def group_dev(m):
        tt, ww, zz = m // 8, (m // 4) % 2, m % 4
        return (zz * 2 + c, zhi * 4 + (2 * c + tt + ww * (2 * tt - 1) + 4) % 4, x)

    def remote(src, dst, ssem, rsem, device):
        return pltpu.make_async_remote_copy(
            src_ref=src, dst_ref=dst, send_sem=ssem, recv_sem=rsem, device_id=device, device_id_type=MESH
        )

    def arrived(dst, rsem):
        pltpu.make_async_copy(dst, dst, rsem).wait()

    loads = [
        pltpu.make_async_copy(wqkv_h, w_s, wsem.at[0]),
        pltpu.make_async_copy(wo_h, w_so, wsem.at[1]),
        pltpu.make_async_copy(tqkv_h, w_t, wsem.at[2]),
        pltpu.make_async_copy(to_h, w_to, wsem.at[3]),
        pltpu.make_async_copy(up_h, w_up, wsem.at[4]),
        pltpu.make_async_copy(dn_h, w_dn, wsem.at[5]),
    ]
    for load in loads:
        load.start()

    bar = pltpu.get_barrier_semaphore()

    def tell(device):
        pl.semaphore_signal(bar, inc=1, device_id=device, device_id_type=MESH)

    def first_peer(i, k):
        return dev(zlo, y // 2, zhi, 2 * c + i, (x + k) % 4)

    for k in range(1, 4):
        tell(xdev(k))
        for i in range(2):
            tell(first_peer(i, k))
    tell(dev(zlo, 1 - c, zhi, y, x))
    for k in range(1, 16):
        tell(group_dev((m_me + k) % 16))

    @pl.when(cross)
    def _():
        tell(dev(zlo, 1 - c, 1 - zhi, y, x))

    @pl.when(jnp.logical_not(at_home))
    def _():
        for i in range(2):
            tell(first_peer(i, 0))
        for z in range(4):
            tell(dev(z, 1 - c, zhi, y, x))
            tell(dev(z, 1 - c, zhi, (2 * (1 - c) + 3 * (y % 2) + 3) % 4, x))

    pl.semaphore_wait(
        bar, 9 + 1 + 15 + 4 + jnp.where(cross, 1, 0) + jnp.where(at_home, 0, 2)
    )

    slot = y % 2

    def first_copy(i, k):
        return remote(lat.at[i], g.at[x, slot], s1.at[i * 4 + k], d1.at[x * 2 + slot], first_peer(i, k))

    for k in (2, 1, 3):
        for i in range(2):
            first_copy(i, k).start()

    @pl.when(at_home)
    def _():
        pltpu.make_async_copy(lat.at[slot], g.at[x, slot], d1.at[x * 2 + slot]).start()
        first_copy(1 - slot, 0).start()

    @pl.when(jnp.logical_not(at_home))
    def _():
        first_copy(0, 0).start()
        first_copy(1, 0).start()

    masks = head_masks()
    order = one_hot(128, 128, lambda r: 16 * ((r % 32) // 4) + 4 * (r // 32) + r % 4)
    chosen = one_hot(32, 128, lambda r: 16 * (r // 4) + 4 * x + r % 4)

    @pl.when(jnp.logical_not(cross))
    def _():
        outr[...] = jnp.zeros_like(outr)

    for s in range(2):
        for xs in range(4):
            arrived(g.at[xs, s], d1.at[xs * 2 + s])
        whole = jnp.concatenate([g[xs, s].astype(F32) for xs in range(4)], axis=1)
        lfull[s * 128 : (s + 1) * 128] = whole.astype(BF16)
        nrm[s * 128 : (s + 1) * 128] = modulate(whole, mod[0:1], mod[1:2])

    loads[0].wait()
    kvo[0] = dot(nrm[...], w_s[1]).astype(BF16)
    kvo[1] = dot(nrm[...], w_s[2]).astype(BF16)
    row_a, row_b = 1 - c, c
    inner = remote(
        kvo.at[:, pl.ds(row_a * 128, 128)], inn, sh.at[0], dh.at[0], dev(zlo, 1 - c, zhi, y, x)
    )
    outer = remote(
        kvo.at[:, pl.ds(row_b * 128, 128)], outr, sh.at[1], dh.at[1], dev(zlo, 1 - c, 1 - zhi, y, x)
    )

    @pl.when(cross)
    def _():
        outer.start()

    inner.start()
    queries = dot(nrm[...], w_s[0]).astype(BF16)
    for s in range(2):
        qb[s] = dot(order, queries[s * 128 : (s + 1) * 128]).astype(BF16)
        lsel[s] = dot(chosen, lfull[s * 128 : (s + 1) * 128]).astype(BF16)
    loads[1].wait()

    def spatial(t, extra, bias):
        q4 = stack_heads(qb[t], masks)
        own = dot_t(q4, kvo[0]) * SCALE
        far = dot_t(q4, extra[0]) * SCALE + bias
        p = softmax(jnp.concatenate([own, far], axis=1))
        o = dot(p[:, :256], kvo[1]) + dot(p[:, 256:], extra[1])
        ps[t] = dot(pick_heads(o, masks), w_so[...]).astype(BF16)

    def spatial_send(n, t, k):
        return remote(
            ps.at[t, pl.ds(((x + k) % 4) * 32, 32)], r4.at[x, t], s4.at[n * 4 + k], d4.at[x * 2 + t], xdev(k)
        )

    arrived(inn, dh.at[0])
    spatial(row_a, inn, 0.0)
    for k in (2, 1, 3):
        spatial_send(0, row_a, k).start()

    @pl.when(cross)
    def _():
        arrived(outr, dh.at[1])

    spatial(row_b, outr, jnp.where(cross, 0.0, -1e30))
    for k in (2, 1, 3):
        spatial_send(1, row_b, k).start()

    for t in (row_a, row_b):
        total = ps[t, pl.ds(x * 32, 32)].astype(F32)
        for k in (1, 3, 2):
            xs = (x + k) % 4
            arrived(r4.at[xs, t], d4.at[xs * 2 + t])
            total = total + r4[xs, t].astype(F32)
        fst[t] = (lsel[t].astype(F32) + mod[2:3] * total).astype(BF16)

    rows = jnp.concatenate([fst[0], fst[1]], axis=0)
    packed = jnp.zeros((256, COVER), F32)
    for j in range(3):
        r = lax.broadcasted_iota(jnp.int32, (256, 64), 0)
        s = lax.broadcasted_iota(jnp.int32, (256, 64), 1)
        sel = jnp.where((r // 16 == s // 4) & ((r % 16) // 4 == j) & (r % 4 == s % 4), 1.0, 0.0).astype(BF16)
        packed = packed + dot(sel, rows[:, j * COVER : (j + 1) * COVER])
    pk[...] = packed.astype(BF16).reshape(16, 16, COVER)

    def spread(k):
        m = (m_me + k) % 16
        return remote(pk.at[m], a2.at[f_me], s5.at[k], d5.at[f_me], group_dev(m))

    for k in range(1, 16):
        spread(k).start()
    a2[f_me] = pk[m_me]
    for k in range(1, 16):
        f = (f_me + k) % 16
        arrived(a2.at[f], d5.at[f])
    flat = a2[...].reshape(256, COVER)
    for j in range(3):
        r = lax.broadcasted_iota(jnp.int32, (64, 256), 0)
        s = lax.broadcasted_iota(jnp.int32, (64, 256), 1)
        sel = jnp.where((s // 16 == r // 4) & ((s % 16) // 4 == j) & (r % 4 == s % 4), 1.0, 0.0).astype(BF16)
        blk[x, :, j * COVER : (j + 1) * COVER] = dot(sel, flat).astype(BF16)

    def gather(buf, ssem, rsem, k):
        return remote(buf.at[x], buf.at[x], ssem.at[k], rsem.at[x], xdev(k))

    for k in (2, 1, 3):
        gather(blk, s6, d6, k).start()
    loads[2].wait()
    loads[3].wait()
    for k in (1, 3, 2):
        xs = (x + k) % 4
        arrived(blk.at[xs], d6.at[xs])
    for xs in range(4):
        nrm[xs * 64 : (xs + 1) * 64] = modulate(blk[xs].astype(F32), mod[3:4], mod[4:5])
    tq = dot(nrm[...], w_t[0]).astype(BF16)
    tk = dot(nrm[...], w_t[1]).astype(BF16)
    tv = dot(nrm[...], w_t[2]).astype(BF16)
    r = lax.broadcasted_iota(jnp.int32, (256, 64), 0)
    s = lax.broadcasted_iota(jnp.int32, (256, 64), 1)
    same = r % 4 == s % 4
    for xs in range(4):
        span = slice(xs * 64, (xs + 1) * 64)
        sc = dot_t(stack_heads(tq[span], masks), tk[span]) * SCALE
        p = softmax(jnp.where(same, sc, -1e30))
        att[span] = pick_heads(dot(p, tv[span]), masks)
    pt[...] = dot(att[...], w_to[...]).astype(BF16).reshape(4, 64, D)

    def reduce_send(k):
        xd = (x + k) % 4
        return remote(pt.at[xd], r7.at[x], s7.at[k], d7.at[x], xdev(k))

    for k in (2, 1, 3):
        reduce_send(k).start()
    total = pt[x].astype(F32)
    for k in (1, 3, 2):
        xs = (x + k) % 4
        arrived(r7.at[xs], d7.at[xs])
        total = total + r7[xs].astype(F32)
    blk2[x] = (blk[x].astype(F32) + mod[5:6] * total).astype(BF16)

    for k in (2, 1, 3):
        gather(blk2, s7b, d7b, k).start()
    loads[4].wait()
    loads[5].wait()
    for k in (1, 3, 2):
        xs = (x + k) % 4
        arrived(blk2.at[xs], d7b.at[xs])
    for xs in range(4):
        nrm[xs * 64 : (xs + 1) * 64] = modulate(blk2[xs].astype(F32), mod[6:7], mod[7:8])

    def mlp_send(n, k):
        xd = (x + k) % 4
        return remote(
            pm.at[n, :, pl.ds(pl.multiple_of(xd * 256, 128), COVER)], r8.at[x, n],
            s8.at[n * 4 + k], d8.at[x * 2 + n], xdev(k),
        )

    for n in range(2):
        span = slice(n * 128, (n + 1) * 128)
        hid[span] = jax.nn.gelu(dot(nrm[span], w_up[...]), approximate=True).astype(BF16)
        pm[n] = dot(hid[span], w_dn[...]).astype(BF16)
        for k in (2, 1, 3):
            mlp_send(n, k).start()

    lanes = pl.ds(pl.multiple_of(x * 256, 128), COVER)
    gate = mod[8:9, lanes]
    parts = []
    for n in range(2):
        total = pm[n, :, lanes].astype(F32)
        for k in (1, 3, 2):
            xs = (x + k) % 4
            arrived(r8.at[xs, n], d8.at[xs * 2 + n])
            total = total + r8[xs, n].astype(F32)
        base = blk2[2 * n : 2 * n + 2, :, lanes].reshape(128, COVER).astype(F32)
        moved = pltpu.roll(base + gate * total, (COVER - 32 * x) % COVER, 1)
        parts.append(moved[:, :PART].astype(BF16))
    turn = one_hot(256, 256, lambda r: 64 * ((r % 16) // 4) + 4 * (r // 16) + r % 4)
    fin[...] = dot(turn, jnp.concatenate(parts, axis=0)).astype(BF16).reshape(16, 16, PART)

    b_me = 4 * w + zlo

    def back(kz, kc):
        zd, cd = (zlo + kz) % 4, (c + kc) % 2
        return remote(
            fin.at[pl.ds((2 * zd + cd) * 2, 2)], o_ref.at[:, pl.ds(b_me * 16, 16)],
            s9.at[kz * 2 + kc], d9.at[b_me], dev(zd, cd, zhi, 2 * c + t_me, x),
        )

    own_out = pltpu.make_async_copy(
        fin.at[pl.ds((2 * zlo + c) * 2, 2)], o_ref.at[:, pl.ds(b_me * 16, 16)], d9.at[b_me]
    )
    for kz in (3, 2, 1, 0):
        for kc in range(2):
            if kz or kc:
                back(kz, kc).start()

    @pl.when(at_home)
    def _():
        own_out.start()

    @pl.when(jnp.logical_not(at_home))
    def _():
        back(0, 0).start()

    for k in range(1, 4):
        for i in range(2):
            first_copy(i, k).wait_send()
        for n, t in enumerate((row_a, row_b)):
            spatial_send(n, t, k).wait_send()
        gather(blk, s6, d6, k).wait_send()
        reduce_send(k).wait_send()
        gather(blk2, s7b, d7b, k).wait_send()
        for n in range(2):
            mlp_send(n, k).wait_send()
    for k in range(1, 16):
        spread(k).wait_send()
    inner.wait_send()

    @pl.when(cross)
    def _():
        outer.wait_send()

    @pl.when(at_home)
    def _():
        first_copy(1 - slot, 0).wait_send()

    @pl.when(jnp.logical_not(at_home))
    def _():
        first_copy(0, 0).wait_send()
        first_copy(1, 0).wait_send()
        back(0, 0).wait_send()

    for kz in range(4):
        for kc in range(2):
            if kz or kc:
                back(kz, kc).wait_send()
    for b in range(8):
        arrived(o_ref.at[:, pl.ds(b * 16, 16)], d9.at[b])


def body(latents, modulation, spatial_qkv, spatial_out, temporal_qkv, temporal_out, mlp_up, mlp_down):
    anywhere = pl.BlockSpec(memory_space=pl.ANY)
    sem = pltpu.SemaphoreType.DMA
    vm = pltpu.VMEM
    out = pl.pallas_call(
        kernel,
        out_shape=jax.ShapeDtypeStruct((2, 128, PART), BF16),
        in_specs=[anywhere, pl.BlockSpec(memory_space=pltpu.VMEM)] + [anywhere] * 6,
        out_specs=anywhere,
        scratch_shapes=[
            vm((3, D, PART), BF16), vm((PART, D), BF16), vm((3, D, PART), BF16), vm((PART, D), BF16),
            vm((D, D), BF16), vm((D, D), BF16),
            vm((4, 2, 128, PART), BF16),
            vm((256, D), BF16),
            vm((256, D), BF16),
            vm((2, 128, PART), BF16),
            vm((2, 256, PART), BF16),
            vm((2, 128, PART), BF16),
            vm((2, 128, PART), BF16),
            vm((2, 128, D), BF16),
            vm((4, 2, 32, D), BF16),
            vm((2, 32, D), BF16),
            vm((2, 32, D), BF16),
            vm((16, 16, COVER), BF16),
            vm((16, 16, COVER), BF16),
            vm((4, 64, D), BF16),
            vm((256, PART), BF16),
            vm((4, 64, D), BF16),
            vm((4, 64, D), BF16),
            vm((4, 64, D), BF16),
            vm((256, D), BF16),
            vm((2, 128, D), BF16),
            vm((4, 2, 128, COVER), BF16),
            vm((16, 16, PART), BF16),
            sem((6,)),
            sem((8,)), sem((8,)), sem((2,)), sem((2,)), sem((8,)), sem((8,)), sem((16,)), sem((16,)),
            sem((4,)), sem((4,)), sem((4,)), sem((4,)), sem((4,)), sem((4,)), sem((8,)), sem((8,)),
            sem((8,)), sem((8,)),
        ],
        compiler_params=pltpu.CompilerParams(
            collective_id=0, has_side_effects=True, vmem_limit_bytes=48 * 2**20
        ),
        name="block",
    )(
        latents.reshape(2, 128, PART), modulation, spatial_qkv, spatial_out, temporal_qkv, temporal_out,
        mlp_up, mlp_down,
    )
    return out.reshape(latents.shape)


def solution(mesh):
    return jax.shard_map(
        body,
        mesh=mesh,
        in_specs=(
            P("tm", "height", None, "head"),
            P(),
            P(None, None, "head"),
            P("head", None),
            P(None, None, "head"),
            P("head", None),
            P(None, "head"),
            P("head", None),
        ),
        out_specs=P("tm", "height", None, "head"),
        check_vma=False,
    )
```

```python
import jax
import jax.numpy as jnp
from jax import lax
from jax.experimental import pallas as pl
from jax.experimental.pallas import tpu as pltpu
from jax.sharding import PartitionSpec as P

D = 1152
HEAD_DIM = 72
PART = 288
COVER = 384
HEADS = 4
EPSILON = 1e-06
SCALE = HEAD_DIM ** (-0.5)
MESH = pl.DeviceIdType.MESH
F32 = jnp.float32
BF16 = jnp.bfloat16
ORDER = [(0, 0), (0, 1), (1, 0), (1, 1), (2, 0), (2, 1), (3, 0), (3, 1), (4, 0), (4, 1), (5, 0), (5, 1)]


def dot(a, b):
    return jnp.dot(a, b, preferred_element_type=F32)


def dot_t(a, b):
    return lax.dot_general(a, b, (((1,), (1,)), ((), ())), preferred_element_type=F32)


def modulate(v, shift, scale):
    mean = jnp.mean(v, axis=-1, keepdims=True)
    cen = v - mean
    var = jnp.mean(cen * cen, axis=-1, keepdims=True)
    return (cen * lax.rsqrt(var + EPSILON) * (1.0 + scale) + shift).astype(BF16)


def grid(rows, cols):
    return (
        lax.broadcasted_iota(jnp.int32, (rows, cols), 0),
        lax.broadcasted_iota(jnp.int32, (rows, cols), 1),
    )


def flags(condition):
    return jnp.where(condition, 1.0, 0.0).astype(BF16)


def lane_masks(width, start):
    lane = lax.broadcasted_iota(jnp.int32, (1, width), 1)
    return [
        jnp.where((lane >= start + HEAD_DIM * h) & (lane < start + HEAD_DIM * (h + 1)), 1.0, 0.0)
        for h in range(HEADS)
    ]


def stack_heads(q, masks):
    return jnp.concatenate([(q * m).astype(BF16) for m in masks], axis=0)


def pick_heads(o, masks):
    n = o.shape[0] // HEADS
    total = o[0:n] * masks[0]
    for h in range(1, HEADS):
        total = total + o[h * n : (h + 1) * n] * masks[h]
    return total[:, PART:].astype(BF16)


def softmax(s):
    top = jnp.max(s, axis=-1, keepdims=True)
    e = jnp.exp(s - top)
    return (e / jnp.sum(e, axis=-1, keepdims=True)).astype(BF16)


def pack_part(v):
    rest = jnp.concatenate([v[32 * k : 32 * k + 32, 256:] for k in range(4)], axis=1)
    return jnp.concatenate([v[:, :128], v[:, 128:256], rest], axis=0)


def unpack_part(v):
    rest = jnp.concatenate([v[256:, 32 * k : 32 * k + 32] for k in range(4)], axis=0)
    return jnp.concatenate([v[:128], v[128:256], rest], axis=1)


def pack_kv(v):
    rest = jnp.concatenate([v[:64, 512:], v[64:, 512:]], axis=1)
    return jnp.concatenate([v[:, 128 * j : 128 * j + 128] for j in range(4)] + [rest], axis=0)


def unpack_kv(v):
    rest = jnp.concatenate([v[512:, :64], v[512:, 64:]], axis=0)
    return jnp.concatenate([v[128 * j : 128 * j + 128] for j in range(4)] + [rest], axis=1)


def kernel(
    lat, mod_h, wqkv_h, wo_h, tqkv_h, to_h, up_h, dn_h, o_ref,
    mod, w_s, w_so, w_t, w_to, w_up, w_dn, w_dp,
    lv, lp, g, lfull, qb, kvf, hp, inn, outr, ps, r4, lsel, pk, a2, blk, pt, r7, blk2, pmp, r8, fin,
    spread_sel, unpack_sel, turn,
    wsem, s1, d1, sh, dh, s4, d4, s5, d5, s6, d6, s7, d7, s7b, d7b, s8, d8, s9, d9, zsem, csem,
):
    tm = lax.axis_index("tm")
    he = lax.axis_index("height")
    x = lax.axis_index("head")
    zlo, c = tm // 2, tm % 2
    zhi, y = he // 4, he % 4
    m_me = 4 * y + zlo
    f_me = 4 * zlo + y
    at_home = y // 2 == c
    away = y // 2 != c
    cross = zhi != c
    row_a, row_b = 1 - c, c
    row_of = (row_a, row_b)

    def dev(zlo, c, zhi, y, x):
        return (zlo * 2 + c, zhi * 4 + y, x)

    def xdev(k):
        return (tm, he, (x + k) % 4)

    def group_dev(m):
        return dev(m % 4, c, zhi, m // 4, x)

    def remote(src, dst, ssem, rsem, device):
        return pltpu.make_async_remote_copy(
            src_ref=src, dst_ref=dst, send_sem=ssem, recv_sem=rsem, device_id=device, device_id_type=MESH
        )

    def arrived(dst, rsem):
        pltpu.make_async_copy(dst, dst, rsem).wait()

    sent = []

    def send(copy):
        copy.start()
        sent.append(copy.wait_send)

    def send_if(condition, copy):
        pl.when(condition)(copy.start)
        sent.append(lambda: pl.when(condition)(copy.wait_send))

    loads = [
        pltpu.make_async_copy(wqkv_h, w_s, wsem.at[0]),
        pltpu.make_async_copy(wo_h, w_so, wsem.at[1]),
        pltpu.make_async_copy(tqkv_h, w_t, wsem.at[2]),
        pltpu.make_async_copy(to_h, w_to, wsem.at[3]),
        pltpu.make_async_copy(up_h, w_up, wsem.at[4]),
        pltpu.make_async_copy(dn_h, w_dn, wsem.at[5]),
        pltpu.make_async_copy(mod_h, mod, wsem.at[6]),
        pltpu.make_async_copy(lat, lv, wsem.at[7]),
    ]
    for k in (7, 6, 0, 1, 5, 2, 3, 4):
        loads[k].start()

    bar = pltpu.get_barrier_semaphore()

    def tell(device):
        pl.semaphore_signal(bar, inc=1, device_id=device, device_id_type=MESH)

    def first_peer(i, k):
        return dev(zlo, y // 2, zhi, 2 * c + i, (x + k) % 4)

    def z_peer(k):
        return dev((zlo + k) % 4, c, zhi, y, x)

    for k in range(1, 4):
        for i in range(2):
            tell(first_peer(i, k))
    for k in range(1, 4):
        tell(xdev(k))
        tell(dev(zlo, c, zhi, (y + k) % 4, x))
        tell(z_peer(k))
    tell(dev(zlo, 1 - c, zhi, y, x))

    @pl.when(cross)
    def _():
        tell(dev(zlo, 1 - c, 1 - zhi, y, x))

    @pl.when(away)
    def _():
        for i in range(2):
            tell(first_peer(i, 0))

    loads[7].wait()
    for i in range(2):
        lp[i] = pack_part(lv[i].astype(F32)).astype(BF16)
    pl.semaphore_wait(bar, 16 + jnp.where(cross, 1, 0) + jnp.where(away, 2, 0))

    slot = y % 2

    def first_copy(i, k):
        return remote(lp.at[i], g.at[x, slot], s1.at[i * 4 + k], d1.at[x * 2 + slot], first_peer(i, k))

    for k in (2, 1, 3):
        for i in range(2):
            send(first_copy(i, k))

    @pl.when(at_home)
    def _():
        pltpu.make_async_copy(lp.at[slot], g.at[x, slot], d1.at[x * 2 + slot]).start()

    send_if(at_home, first_copy(1 - slot, 0))
    for i in range(2):
        send_if(away, first_copy(i, 0))

    for k in range(1, 4):
        pl.semaphore_signal(zsem, inc=1, device_id=z_peer(k), device_id_type=MESH)

    q_masks = lane_masks(PART, 0)
    v_masks = lane_masks(2 * PART, PART)
    r, s = grid(256, 160)
    spread_sel[...] = flags((r // 16 == (s % 32) // 2) & ((r % 16) // 2 == s // 32) & (r % 2 == s % 2))
    r, s = grid(160, 256)
    unpack_sel[...] = flags((r % 16 == s // 16) & (r // 32 == (s % 16) // 2) & ((r % 32) // 16 == s % 2))
    r, s = grid(128, 128)
    order = flags(s == 8 * ((r % 32) // 2) + 2 * (r // 32) + r % 2)
    turn[...] = flags(s == 32 * ((r % 8) // 2) + 16 * (r % 2) + r // 8)
    r, s = grid(32, 128)
    chosen = flags(s == 8 * (r // 2) + 2 * x + r % 2)

    @pl.when(jnp.logical_not(cross))
    def _():
        outr[...] = jnp.zeros_like(outr)

    loads[5].wait()

    def reorder(i, _):
        span = pl.ds(pl.multiple_of(i * 128, 128), 128)
        v = w_dn[span, :].astype(F32)
        pieces = [v[:, PART * k : PART * k + 256] for k in range(4)]
        pieces += [v[:, PART * k + 256 : PART * k + PART] for k in range(4)]
        w_dp[span, :] = jnp.concatenate(pieces, axis=1).astype(BF16)
        return 0

    lax.fori_loop(0, 9, reorder, 0)
    loads[6].wait()
    loads[0].wait()

    def prepare(t):
        for xs in range(4):
            arrived(g.at[xs, t], d1.at[xs * 2 + t])
        whole = jnp.concatenate([unpack_part(g[xs, t].astype(F32)) for xs in range(4)], axis=1)
        lfull[t] = whole.astype(BF16)
        normed = modulate(whole, mod[0:1], mod[1:2])
        kv = dot_t(normed, w_s[PART:])
        kvf[t] = kv.astype(BF16)
        hp[t] = pack_kv(kv).astype(BF16)
        return normed

    normed_b = prepare(row_b)
    outer = remote(hp.at[row_b], outr, sh.at[1], dh.at[1], dev(zlo, 1 - c, 1 - zhi, y, x))
    send_if(cross, outer)
    normed_a = prepare(row_a)
    inner = remote(hp.at[row_a], inn, sh.at[0], dh.at[0], dev(zlo, 1 - c, zhi, y, x))
    send(inner)
    for t, normed in ((row_a, normed_a), (row_b, normed_b)):
        qb[t] = dot(order, dot_t(normed, w_s[:PART]).astype(BF16)).astype(BF16)
    loads[1].wait()

    def spatial(n, extra, bias):
        q4 = stack_heads(qb[row_of[n]].astype(F32), q_masks)
        kv = kvf[...].reshape(256, 2 * PART)
        far = unpack_kv(extra[...].astype(F32)).astype(BF16)
        s_own = dot_t(q4, kv[:, :PART]) * SCALE
        s_far = dot_t(q4, far[:, :PART]) * SCALE + bias
        p = softmax(jnp.concatenate([s_own, s_far], axis=1))
        o = pick_heads(dot(p[:, :256], kv) + dot(p[:, 256:], far), v_masks)
        ps[n] = dot(o, w_so[...]).astype(BF16)
        for k in (2, 1, 3):
            send(remote(
                ps.at[n, pl.ds(((x + k) % 4) * 32, 32)], r4.at[n, x], s4.at[n * 4 + k], d4.at[n * 4 + x], xdev(k)
            ))

    arrived(inn, dh.at[0])
    spatial(0, inn, 0.0)
    for n in range(2):
        lsel[n] = dot(chosen, lfull[row_of[n]]).astype(BF16)

    @pl.when(cross)
    def _():
        arrived(outr, dh.at[1])

    spatial(1, outr, jnp.where(cross, 0.0, -1e30))
    pl.semaphore_wait(zsem, 3)

    def gather(buf, n, ssem, rsem):
        for k in (2, 1, 3):
            send(remote(buf.at[n, x], buf.at[n, x], ssem.at[n * 4 + k], rsem.at[n * 4 + x], xdev(k)))

    def others(buf, n, rsem):
        for k in (1, 3, 2):
            xs = (x + k) % 4
            arrived(buf.at[n, xs], rsem.at[n * 4 + xs])

    def summed(mine, buf, n, rsem):
        total = mine.astype(F32)
        for k in (1, 3, 2):
            xs = (x + k) % 4
            arrived(buf.at[n, xs], rsem.at[n * 4 + xs])
            total = total + buf[n, xs].astype(F32)
        return total

    def stage_spread(n):
        total = summed(ps[n, pl.ds(x * 32, 32)], r4, n, d4)
        rows = (lsel[n].astype(F32) + mod[2:3] * total).astype(BF16)
        rows = jnp.concatenate([rows, jnp.zeros((32, 128), BF16)], axis=1)
        tall = jnp.concatenate([rows[:, 256 * j : 256 * j + 256] for j in range(5)], axis=0)
        pk[n] = dot(spread_sel[...], tall).astype(BF16).reshape(16, 16, 256)
        for k in range(1, 16):
            m = (m_me + k) % 16
            send(remote(pk.at[n, m], a2.at[n, f_me], s5.at[n * 16 + k], d5.at[n * 16 + f_me], group_dev(m)))
        a2[n, f_me] = pk[n, m_me]

    def stage_gather(n):
        for k in range(1, 16):
            f = (f_me + k) % 16
            arrived(a2.at[n, f], d5.at[n * 16 + f])
        tall = dot(unpack_sel[...], a2[n].reshape(256, 256)).astype(BF16)
        wide = jnp.concatenate([tall[32 * j : 32 * j + 32] for j in range(5)], axis=1)
        blk[n, x] = wide[:, :D]
        gather(blk, n, s6, d6)

    def stage_temporal(n):
        others(blk, n, d6)
        normed = modulate(blk[n].reshape(128, D).astype(F32), mod[3:4], mod[4:5])
        q4 = stack_heads(dot_t(normed, w_t[:PART]).astype(BF16).astype(F32), q_masks)
        kv = dot_t(normed, w_t[PART:]).astype(BF16)
        r, s = grid(512, 128)
        sc = jnp.where((r % 128) // 16 == s // 16, dot_t(q4, kv[:, :PART]) * SCALE, -1e30)
        o = pick_heads(dot(softmax(sc), kv), v_masks)
        pt[n] = dot(o, w_to[...]).astype(BF16).reshape(4, 32, D)
        for k in (2, 1, 3):
            send(remote(pt.at[n, (x + k) % 4], r7.at[n, x], s7.at[n * 4 + k], d7.at[n * 4 + x], xdev(k)))

    def stage_second(n):
        total = summed(pt[n, x], r7, n, d7)
        blk2[n, x] = (blk[n, x].astype(F32) + mod[5:6] * total).astype(BF16)
        gather(blk2, n, s7b, d7b)

    def stage_mlp(n):
        others(blk2, n, d7b)
        normed = modulate(blk2[n].reshape(128, D).astype(F32), mod[6:7], mod[7:8])
        hidden = jax.nn.gelu(dot(normed, w_up[...]), approximate=True).astype(BF16)
        out = dot(hidden, w_dp[...])
        for xd in range(4):
            rest = [out[32 * k : 32 * k + 32, 1024 + 32 * xd : 1056 + 32 * xd] for k in range(4)]
            pmp[n, xd] = jnp.concatenate(
                [out[:, 256 * xd : 256 * xd + 128], out[:, 256 * xd + 128 : 256 * xd + 256],
                 jnp.concatenate(rest, axis=1)], axis=0,
            ).astype(BF16)
        for k in (2, 1, 3):
            send(remote(pmp.at[n, (x + k) % 4], r8.at[n, x], s8.at[n * 4 + k], d8.at[n * 4 + x], xdev(k)))

    def stage_return(n):
        lanes = pl.ds(pl.multiple_of(x * 256, 128), COVER)
        shift = (COVER - 32 * x) % COVER
        gate = pltpu.roll(jnp.broadcast_to(mod[8:9, lanes], (8, COVER)), shift, 1)[:1, :PART]
        base = pltpu.roll(blk2[n, :, :, lanes].reshape(128, COVER).astype(F32), shift, 1)[:, :PART]
        total = unpack_part(summed(pmp[n, x], r8, n, d8))
        out = (base + gate * total).astype(BF16)
        fin[n] = dot(turn[...], out).astype(BF16).reshape(8, 16, PART)
        y_to = 2 * c + row_of[n]

        def back(kz, kc):
            zd, cd = (zlo + kz) % 4, (c + kc) % 2
            return remote(
                fin.at[n, 2 * zd + cd], o_ref.at[m_me], s9.at[n * 8 + kz * 2 + kc], d9.at[m_me], dev(zd, cd, zhi, y_to, x)
            )

        for kz in (3, 2, 1, 0):
            for kc in range(2):
                if kz or kc:
                    send(back(kz, kc))
        here = y_to == y
        send_if(jnp.logical_not(here), back(0, 0))

        @pl.when(here)
        def _():
            pltpu.make_async_copy(fin.at[n, 2 * zlo + c], o_ref.at[m_me], d9.at[m_me]).start()

    for k in (2, 3, 4):
        loads[k].wait()
    stages = (stage_spread, stage_gather, stage_temporal, stage_second, stage_mlp, stage_return)
    for k, n in ORDER:
        stages[k](n)
        if (k, n) == (1, 1):
            pl.semaphore_signal(csem, inc=1, device_id=dev(zlo, 1 - c, zhi, y, x), device_id_type=MESH)
        if (k, n) == (4, 0):
            pl.semaphore_wait(csem, 1)

    for done in sent:
        done()
    for m in range(16):
        arrived(o_ref.at[m], d9.at[m])


def body(latents, modulation, spatial_qkv, spatial_out, temporal_qkv, temporal_out, mlp_up, mlp_down):
    anywhere = pl.BlockSpec(memory_space=pl.ANY)
    sem = pltpu.SemaphoreType.DMA

    def vm(*shape):
        return pltpu.VMEM(shape, BF16)

    out = pl.pallas_call(
        kernel,
        out_shape=jax.ShapeDtypeStruct((16, 16, PART), BF16),
        in_specs=[anywhere] * 8,
        out_specs=anywhere,
        scratch_shapes=[
            pltpu.VMEM((9, D), F32),
            vm(3 * PART, D), vm(PART, D), vm(3 * PART, D), vm(PART, D), vm(D, D), vm(D, D), vm(D, D),
            vm(2, 128, PART),
            vm(2, PART, 128),
            vm(4, 2, PART, 128),
            vm(2, 128, D),
            vm(2, 128, PART),
            vm(2, 128, 2 * PART),
            vm(2, 2 * PART, 128),
            vm(2 * PART, 128),
            vm(2 * PART, 128),
            vm(2, 128, D),
            vm(2, 4, 32, D),
            vm(2, 32, D),
            vm(2, 16, 16, 256),
            vm(2, 16, 16, 256),
            vm(2, 4, 32, D),
            vm(2, 4, 32, D),
            vm(2, 4, 32, D),
            vm(2, 4, 32, D),
            vm(2, 4, PART, 128),
            vm(2, 4, PART, 128),
            vm(2, 8, 16, PART),
            vm(256, 160), vm(160, 256), vm(128, 128),
            sem((8,)),
            sem((8,)), sem((8,)), sem((2,)), sem((2,)), sem((8,)), sem((8,)), sem((32,)), sem((32,)),
            sem((8,)), sem((8,)), sem((8,)), sem((8,)), sem((8,)), sem((8,)), sem((8,)), sem((8,)),
            sem((16,)), sem((16,)),
            pltpu.SemaphoreType.REGULAR, pltpu.SemaphoreType.REGULAR,
        ],
        compiler_params=pltpu.CompilerParams(
            collective_id=0, has_side_effects=True, vmem_limit_bytes=60 * 2**20
        ),
        name="block",
    )(
        latents.reshape(2, 128, PART), modulation,
        jnp.swapaxes(spatial_qkv, 1, 2).reshape(3 * PART, D), spatial_out,
        jnp.swapaxes(temporal_qkv, 1, 2).reshape(3 * PART, D), temporal_out, mlp_up, mlp_down,
    )
    return out.reshape(16, 2, 8, PART).transpose(1, 0, 2, 3).reshape(latents.shape)


def solution(mesh):
    return jax.shard_map(
        body,
        mesh=mesh,
        in_specs=(
            P("tm", "height", None, "head"),
            P(),
            P(None, None, "head"),
            P("head", None),
            P(None, None, "head"),
            P("head", None),
            P(None, "head"),
            P("head", None),
        ),
        out_specs=P("tm", "height", None, "head"),
        check_vma=False,
    )
```

```python
import jax
import jax.numpy as jnp
from jax import lax
from jax.experimental import pallas as pl
from jax.experimental.pallas import tpu as pltpu
from jax.sharding import PartitionSpec as P

D = 1152
HEAD_DIM = 72
PART = 288
COVER = 384
HEADS = 4
EPSILON = 1e-06
SCALE = HEAD_DIM ** (-0.5)
MESH = pl.DeviceIdType.MESH
F32 = jnp.float32
BF16 = jnp.bfloat16
CUT = 1
RUN = 32 // CUT
ORDER = [(k, n, 0) for k in range(6) for n in range(2)]


def dot(a, b):
    return jnp.dot(a, b, preferred_element_type=F32)


def dot_t(a, b):
    return lax.dot_general(a, b, (((1,), (1,)), ((), ())), preferred_element_type=F32)


def modulate(v, shift, scale):
    mean = jnp.mean(v, axis=-1, keepdims=True)
    cen = v - mean
    var = jnp.mean(cen * cen, axis=-1, keepdims=True)
    return (cen * lax.rsqrt(var + EPSILON) * (1.0 + scale) + shift).astype(BF16)


def grid(rows, cols):
    return (
        lax.broadcasted_iota(jnp.int32, (rows, cols), 0),
        lax.broadcasted_iota(jnp.int32, (rows, cols), 1),
    )


def flags(condition):
    return jnp.where(condition, 1.0, 0.0).astype(BF16)


def lane_masks(width, start):
    lane = lax.broadcasted_iota(jnp.int32, (1, width), 1)
    return [
        jnp.where((lane >= start + HEAD_DIM * h) & (lane < start + HEAD_DIM * (h + 1)), 1.0, 0.0)
        for h in range(HEADS)
    ]


def stack_heads(q, masks):
    return jnp.concatenate([(q * m).astype(BF16) for m in masks], axis=0)


def pick_heads(o, masks):
    n = o.shape[0] // HEADS
    total = o[0:n] * masks[0]
    for h in range(1, HEADS):
        total = total + o[h * n : (h + 1) * n] * masks[h]
    return total[:, PART:].astype(BF16)


def softmax(s):
    top = jnp.max(s, axis=-1, keepdims=True)
    e = jnp.exp(s - top)
    return (e / jnp.sum(e, axis=-1, keepdims=True)).astype(BF16)


def pack_part(v):
    rest = jnp.concatenate([v[32 * k : 32 * k + 32, 256:] for k in range(4)], axis=1)
    return jnp.concatenate([v[:, :128], v[:, 128:256], rest], axis=0)


def unpack_part(v):
    rest = jnp.concatenate([v[256:, 32 * k : 32 * k + 32] for k in range(4)], axis=0)
    return jnp.concatenate([v[:128], v[128:256], rest], axis=1)


def pack_kv(v):
    rest = jnp.concatenate([v[:64, 512:], v[64:, 512:]], axis=1)
    return jnp.concatenate([v[:, 128 * j : 128 * j + 128] for j in range(4)] + [rest], axis=0)


def unpack_kv(v):
    rest = jnp.concatenate([v[512:, :64], v[512:, 64:]], axis=0)
    return jnp.concatenate([v[128 * j : 128 * j + 128] for j in range(4)] + [rest], axis=1)


def kernel(
    lat, mod_h, wqkv_h, wo_h, tqkv_h, to_h, up_h, dn_h, o_ref,
    mod, w_s, w_so, w_t, w_to, w_up, w_dn, w_dp, c_s, c_t,
    lv, lp, g, lfull, qb, kvf, hp, inn, outr, ps, r4, lsel, pk, a2, blk, pt, r7, blk2, pmp, r8, fin,
    spread_sel, unpack_sel, turn,
    wsem, s1, d1, sh, dh, s4, d4, s5, d5, s6, d6, s7, d7, s7b, d7b, s8, d8, s9, d9, zsem, ysem, xsem, csem,
):
    tm = lax.axis_index("tm")
    he = lax.axis_index("height")
    x = lax.axis_index("head")
    zlo, c = tm // 2, tm % 2
    zhi, y = he // 4, he % 4
    m_me = 4 * y + zlo
    f_me = 4 * zlo + y
    at_home = y // 2 == c
    away = y // 2 != c
    cross = zhi != c
    row_a, row_b = 1 - c, c
    row_of = (row_a, row_b)

    def dev(zlo, c, zhi, y, x):
        return (zlo * 2 + c, zhi * 4 + y, x)

    def xdev(k):
        return (tm, he, (x + k) % 4)

    def group_dev(m):
        return dev(m % 4, c, zhi, m // 4, x)

    def remote(src, dst, ssem, rsem, device):
        return pltpu.make_async_remote_copy(
            src_ref=src, dst_ref=dst, send_sem=ssem, recv_sem=rsem, device_id=device, device_id_type=MESH
        )

    def arrived(dst, rsem):
        pltpu.make_async_copy(dst, dst, rsem).wait()

    sent = []

    def send(copy):
        copy.start()
        sent.append(copy.wait_send)

    def send_if(condition, copy):
        pl.when(condition)(copy.start)
        sent.append(lambda: pl.when(condition)(copy.wait_send))

    loads = [
        pltpu.make_async_copy(wqkv_h, w_s, wsem.at[0]),
        pltpu.make_async_copy(wo_h, w_so, wsem.at[1]),
        pltpu.make_async_copy(tqkv_h, w_t, wsem.at[2]),
        pltpu.make_async_copy(to_h, w_to, wsem.at[3]),
        pltpu.make_async_copy(up_h, w_up, wsem.at[4]),
        pltpu.make_async_copy(dn_h, w_dn, wsem.at[5]),
        pltpu.make_async_copy(mod_h, mod, wsem.at[6]),
        pltpu.make_async_copy(lat, lv, wsem.at[7]),
    ]
    for k in (7, 6, 0, 1, 5, 2, 3, 4):
        loads[k].start()

    bar = pltpu.get_barrier_semaphore()

    def tell(device):
        pl.semaphore_signal(bar, inc=1, device_id=device, device_id_type=MESH)

    def first_peer(i, k):
        return dev(zlo, y // 2, zhi, 2 * c + i, (x + k) % 4)

    z_near = zlo + 1 - 2 * (zlo % 2)
    z_far = (3 - zlo, (zlo + 2) % 4, z_near, zlo)

    def z_dev(z):
        return dev(z, c, zhi, y, x)

    for k in range(1, 4):
        for i in range(2):
            tell(first_peer(i, k))
    for k in range(1, 4):
        tell(xdev(k))
        tell(dev(zlo, c, zhi, (y + k) % 4, x))
    tell(dev(zlo, 1 - c, zhi, y, x))

    for k in range(1, 4):
        pl.when(zlo + k < 4)(lambda k=k: tell(z_dev(zlo + k)))
    cross_dev = dev(zlo, 1 - c, 1 - zhi, y, x)
    pl.when(cross & (zhi == 0))(lambda: tell(cross_dev))

    @pl.when(away)
    def _():
        for i in range(2):
            tell(first_peer(i, 0))

    loads[7].wait()
    for i in range(2):
        lp[i] = pack_part(lv[i].astype(F32)).astype(BF16)
    pl.semaphore_wait(bar, 13 + zlo + jnp.where(cross & (zhi == 1), 1, 0) + jnp.where(away, 2, 0))

    slot = y % 2

    def first_copy(i, k):
        return remote(lp.at[i], g.at[x, slot], s1.at[i * 4 + k], d1.at[x * 2 + slot], first_peer(i, k))

    for k in (2, 1, 3):
        for i in range(2):
            send(first_copy(i, k))

    @pl.when(at_home)
    def _():
        pltpu.make_async_copy(lp.at[slot], g.at[x, slot], d1.at[x * 2 + slot]).start()

    send_if(at_home, first_copy(1 - slot, 0))
    for i in range(2):
        send_if(away, first_copy(i, 0))

    def answer(semaphore, device):
        pl.semaphore_signal(semaphore, inc=1, device_id=device, device_id_type=MESH)

    for k in range(1, 4):
        pl.when(zlo >= k)(lambda k=k: answer(zsem, z_dev(zlo - k)))
    pl.when(cross & (zhi == 1))(lambda: answer(xsem, cross_dev))

    q_masks = lane_masks(PART, 0)
    v_masks = lane_masks(2 * PART, PART)
    r, s = grid(256, 160)
    spread_sel[...] = flags((r // 16 == (s % 32) // 2) & ((r % 16) // 2 == s // 32) & (r % 2 == s % 2))
    r, s = grid(160, 256)
    unpack_sel[...] = flags((r % 16 == s // 16) & (r // 32 == (s % 16) // 2) & ((r % 32) // 16 == s % 2))
    r, s = grid(128, 128)
    order = flags(s == 8 * ((r % 32) // 2) + 2 * (r // 32) + r % 2)
    if CUT == 1:
        turn[...] = flags(s == 32 * ((r % 8) // 2) + 16 * (r % 2) + r // 8)
    else:
        turn[...] = flags(s == 64 * (r % 2) + 16 * ((r % 8) // 2) + r // 8)
    r, s = grid(32, 128)
    chosen = flags(s == 8 * (r // 2) + 2 * x + r % 2)

    @pl.when(jnp.logical_not(cross))
    def _():
        outr[...] = jnp.zeros_like(outr)

    loads[5].wait()

    def reorder(i, _):
        span = pl.ds(pl.multiple_of(i * 128, 128), 128)
        v = w_dn[span, :].astype(F32)
        pieces = [v[:, PART * k : PART * k + 256] for k in range(4)]
        pieces += [v[:, PART * k + 256 : PART * k + PART] for k in range(4)]
        w_dp[span, :] = jnp.concatenate(pieces, axis=1).astype(BF16)
        return 0

    lax.fori_loop(0, 9, reorder, 0)
    loads[6].wait()

    def turn_over(source, target):
        def step(i, _):
            span = pl.ds(pl.multiple_of(i * 128, 128), 128)
            v = source[:, span].astype(F32)
            v = jnp.concatenate([v[PART:], v[:PART]], axis=0)
            target[span, :] = v.T.astype(BF16)
            return 0

        lax.fori_loop(0, 9, step, 0)

    loads[0].wait()
    turn_over(w_s, c_s)
    loads[2].wait()
    turn_over(w_t, c_t)

    def prepare(t):
        for xs in range(4):
            arrived(g.at[xs, t], d1.at[xs * 2 + t])
        whole = jnp.concatenate([unpack_part(g[xs, t].astype(F32)) for xs in range(4)], axis=1)
        lfull[t] = whole.astype(BF16)
        normed = modulate(whole, mod[0:1], mod[1:2])
        kv = dot(normed, c_s[:, : 2 * PART])
        kvf[t] = kv.astype(BF16)
        hp[t] = pack_kv(kv).astype(BF16)
        return normed

    normed_b = prepare(row_b)
    pl.when(cross & (zhi == 0))(lambda: pl.semaphore_wait(xsem, 1))
    outer = remote(hp.at[row_b], outr, sh.at[1], dh.at[1], cross_dev)
    send_if(cross, outer)
    normed_a = prepare(row_a)
    inner = remote(hp.at[row_a], inn, sh.at[0], dh.at[0], dev(zlo, 1 - c, zhi, y, x))
    send(inner)
    for t, normed in ((row_a, normed_a), (row_b, normed_b)):
        qb[t] = dot(order, dot(normed, c_s[:, 2 * PART :]).astype(BF16)).astype(BF16)
    loads[1].wait()

    def spatial(n, extra, bias):
        q4 = stack_heads(qb[row_of[n]].astype(F32), q_masks)
        kv = kvf[...].reshape(256, 2 * PART)
        far = unpack_kv(extra[...].astype(F32)).astype(BF16)
        s_own = dot_t(q4, kv[:, :PART]) * SCALE
        s_far = dot_t(q4, far[:, :PART]) * SCALE + bias
        p = softmax(jnp.concatenate([s_own, s_far], axis=1))
        o = pick_heads(dot(p[:, :256], kv) + dot(p[:, 256:], far), v_masks)
        ps[n] = dot(o, w_so[...]).astype(BF16)
        for k in (2, 1, 3):
            send(remote(
                ps.at[n, pl.ds(((x + k) % 4) * 32, 32)], r4.at[n, x], s4.at[n * 4 + k], d4.at[n * 4 + x], xdev(k)
            ))

    pl.when(zlo < 3)(lambda: pl.semaphore_wait(zsem, 3 - zlo))
    for k in range(1, 4):
        pl.when(zlo + k < 4)(lambda k=k: answer(ysem, z_dev(zlo + k)))
    arrived(inn, dh.at[0])
    spatial(0, inn, 0.0)
    for n in range(2):
        lsel[n] = dot(chosen, lfull[row_of[n]]).astype(BF16)

    @pl.when(cross)
    def _():
        arrived(outr, dh.at[1])

    spatial(1, outr, jnp.where(cross, 0.0, -1e30))
    pl.when(zlo > 0)(lambda: pl.semaphore_wait(ysem, zlo))

    def gather(buf, i, ssem, rsem):
        for k in (2, 1, 3):
            send(remote(buf.at[i, x], buf.at[i, x], ssem.at[i * 4 + k], rsem.at[i * 4 + x], xdev(k)))

    def others(buf, i, rsem):
        for k in (1, 3, 2):
            xs = (x + k) % 4
            arrived(buf.at[i, xs], rsem.at[i * 4 + xs])

    def summed(mine, buf, i, rsem):
        total = mine.astype(F32)
        for k in (1, 3, 2):
            xs = (x + k) % 4
            arrived(buf.at[i, xs], rsem.at[i * 4 + xs])
            total = total + buf[i, xs].astype(F32)
        return total

    def stage_spread(n, u):
        total = summed(ps[n, pl.ds(x * 32, 32)], r4, n, d4)
        rows = (lsel[n].astype(F32) + mod[2:3] * total).astype(BF16)
        rows = jnp.concatenate([rows, jnp.zeros((32, 128), BF16)], axis=1)
        tall = jnp.concatenate([rows[:, 256 * j : 256 * j + 256] for j in range(5)], axis=0)
        pk[n] = dot(spread_sel[...], tall).astype(BF16).reshape(16, 16, 256)
        for j in range(4):
            for k in (2, 1, 3, 0):
                if j < 3 or k:
                    m = 4 * ((y + k) % 4) + z_far[j]
                    send(remote(
                        pk.at[n, m], a2.at[n, f_me], s5.at[n * 16 + 4 * j + k], d5.at[n * 16 + f_me], group_dev(m)
                    ))
        a2[n, f_me] = pk[n, m_me]

    def stage_gather(n, u):
        for k in range(1, 16):
            f = (f_me + k) % 16
            arrived(a2.at[n, f], d5.at[n * 16 + f])
        tall = dot(unpack_sel[...], a2[n].reshape(256, 256)).astype(BF16)
        wide = jnp.concatenate([tall[32 * j : 32 * j + 32] for j in range(5)], axis=1)
        for v in range(CUT):
            blk[n * CUT + v, x] = wide[v * RUN : (v + 1) * RUN, :D]
            gather(blk, n * CUT + v, s6, d6)

    def stage_temporal(n, u):
        i = n * CUT + u
        others(blk, i, d6)
        normed = modulate(blk[i].reshape(4 * RUN, D).astype(F32), mod[3:4], mod[4:5])
        qkv = dot(normed, c_t[...])
        q4 = stack_heads(qkv[:, 2 * PART :].astype(BF16).astype(F32), q_masks)
        kv = qkv[:, : 2 * PART].astype(BF16)
        r, s = grid(16 * RUN, 4 * RUN)
        sc = jnp.where((r % (4 * RUN)) // 16 == s // 16, dot_t(q4, kv[:, :PART]) * SCALE, -1e30)
        o = pick_heads(dot(softmax(sc), kv), v_masks)
        pt[i] = dot(o, w_to[...]).astype(BF16).reshape(4, RUN, D)
        for k in (2, 1, 3):
            send(remote(pt.at[i, (x + k) % 4], r7.at[i, x], s7.at[i * 4 + k], d7.at[i * 4 + x], xdev(k)))

    def stage_second(n, u):
        i = n * CUT + u
        total = summed(pt[i, x], r7, i, d7)
        blk2[i, x] = (blk[i, x].astype(F32) + mod[5:6] * total).astype(BF16)
        gather(blk2, i, s7b, d7b)

    def stage_mlp(n, u):
        for v in range(CUT):
            others(blk2, n * CUT + v, d7b)
        normed = modulate(blk2[n * CUT : (n + 1) * CUT].reshape(128, D).astype(F32), mod[6:7], mod[7:8])
        hidden = jax.nn.gelu(dot(normed, w_up[...]), approximate=True).astype(BF16)
        out = dot(hidden, w_dp[...])
        for xd in range(4):
            rest = [out[32 * k : 32 * k + 32, 1024 + 32 * xd : 1056 + 32 * xd] for k in range(4)]
            pmp[n, xd] = jnp.concatenate(
                [out[:, 256 * xd : 256 * xd + 128], out[:, 256 * xd + 128 : 256 * xd + 256],
                 jnp.concatenate(rest, axis=1)], axis=0,
            ).astype(BF16)
        for k in (2, 1, 3):
            send(remote(pmp.at[n, (x + k) % 4], r8.at[n, x], s8.at[n * 4 + k], d8.at[n * 4 + x], xdev(k)))

    def stage_return(n, u):
        lanes = pl.ds(pl.multiple_of(x * 256, 128), COVER)
        shift = (COVER - 32 * x) % COVER
        gate = pltpu.roll(jnp.broadcast_to(mod[8:9, lanes], (8, COVER)), shift, 1)[:1, :PART]
        base = pltpu.roll(blk2[n * CUT : (n + 1) * CUT, :, :, lanes].reshape(128, COVER).astype(F32), shift, 1)[:, :PART]
        total = unpack_part(summed(pmp[n, x], r8, n, d8))
        out = (base + gate * total).astype(BF16)
        fin[n] = dot(turn[...], out).astype(BF16).reshape(8, 16, PART)
        y_to = 2 * c + row_of[n]

        def back(j, kc):
            zd, cd = z_far[j], (c + kc) % 2
            return remote(
                fin.at[n, 2 * zd + cd], o_ref.at[m_me], s9.at[n * 8 + j * 2 + kc], d9.at[m_me], dev(zd, cd, zhi, y_to, x)
            )

        for j in range(4):
            for kc in range(2):
                if j < 3 or kc:
                    send(back(j, kc))
        here = y_to == y
        send_if(jnp.logical_not(here), back(3, 0))

        @pl.when(here)
        def _():
            pltpu.make_async_copy(fin.at[n, 2 * zlo + c], o_ref.at[m_me], d9.at[m_me]).start()

    for k in (3, 4):
        loads[k].wait()
    stages = (stage_spread, stage_gather, stage_temporal, stage_second, stage_mlp, stage_return)
    for k, n, u in ORDER:
        stages[k](n, u)
        if (k, n) == (1, 1):
            pl.semaphore_signal(csem, inc=1, device_id=dev(zlo, 1 - c, zhi, y, x), device_id_type=MESH)
        if (k, n) == (4, 0):
            pl.semaphore_wait(csem, 1)

    for done in sent:
        done()
    for m in range(16):
        arrived(o_ref.at[m], d9.at[m])


def body(latents, modulation, spatial_qkv, spatial_out, temporal_qkv, temporal_out, mlp_up, mlp_down):
    anywhere = pl.BlockSpec(memory_space=pl.ANY)
    sem = pltpu.SemaphoreType.DMA

    def vm(*shape):
        return pltpu.VMEM(shape, BF16)

    out = pl.pallas_call(
        kernel,
        out_shape=pltpu.VMEM((16, 16, PART), BF16),
        in_specs=[anywhere] * 8,
        out_specs=anywhere,
        scratch_shapes=[
            pltpu.VMEM((9, D), F32),
            vm(3 * PART, D), vm(PART, D), vm(3 * PART, D), vm(PART, D), vm(D, D), vm(D, D), vm(D, D),
            vm(D, 3 * PART), vm(D, 3 * PART),
            vm(2, 128, PART),
            vm(2, PART, 128),
            vm(4, 2, PART, 128),
            vm(2, 128, D),
            vm(2, 128, PART),
            vm(2, 128, 2 * PART),
            vm(2, 2 * PART, 128),
            vm(2 * PART, 128),
            vm(2 * PART, 128),
            vm(2, 128, D),
            vm(2, 4, 32, D),
            vm(2, 32, D),
            vm(2, 16, 16, 256),
            vm(2, 16, 16, 256),
            vm(2 * CUT, 4, RUN, D),
            vm(2 * CUT, 4, RUN, D),
            vm(2 * CUT, 4, RUN, D),
            vm(2 * CUT, 4, RUN, D),
            vm(2, 4, PART, 128),
            vm(2, 4, PART, 128),
            vm(2, 8, 16, PART),
            vm(256, 160), vm(160, 256), vm(128, 128),
            sem((8,)),
            sem((8,)), sem((8,)), sem((2,)), sem((2,)), sem((8,)), sem((8,)), sem((32,)), sem((32,)),
            sem((8 * CUT,)), sem((8 * CUT,)), sem((8 * CUT,)), sem((8 * CUT,)), sem((8 * CUT,)), sem((8 * CUT,)),
            sem((8,)), sem((8,)), sem((16,)), sem((16,)),
            pltpu.SemaphoreType.REGULAR, pltpu.SemaphoreType.REGULAR,
            pltpu.SemaphoreType.REGULAR, pltpu.SemaphoreType.REGULAR,
        ],
        compiler_params=pltpu.CompilerParams(
            collective_id=0, has_side_effects=True, vmem_limit_bytes=60 * 2**20
        ),
        name="block",
    )(
        latents.reshape(2, 128, PART), modulation,
        jnp.swapaxes(spatial_qkv, 1, 2).reshape(3 * PART, D), spatial_out,
        jnp.swapaxes(temporal_qkv, 1, 2).reshape(3 * PART, D), temporal_out, mlp_up, mlp_down,
    )
    return out.reshape(16, 2, 8, PART).transpose(1, 0, 2, 3).reshape(latents.shape)


def solution(mesh):
    return jax.shard_map(
        body,
        mesh=mesh,
        in_specs=(
            P("tm", "height", None, "head"),
            P(),
            P(None, None, "head"),
            P("head", None),
            P(None, None, "head"),
            P("head", None),
            P(None, "head"),
            P("head", None),
        ),
        out_specs=P("tm", "height", None, "head"),
        check_vma=False,
    )
```

```python
import jax
import jax.numpy as jnp
from jax import lax
from jax.experimental import pallas as pl
from jax.experimental.pallas import tpu as pltpu
from jax.sharding import PartitionSpec as P

D = 1152
HEAD_DIM = 72
PART = 288
COVER = 384
HEADS = 4
EPSILON = 1e-06
SCALE = HEAD_DIM ** (-0.5)
MESH = pl.DeviceIdType.MESH
F32 = jnp.float32
BF16 = jnp.bfloat16
CUT = 1
RUN = 32 // CUT
ORDER = [(k, n, 0) for k in range(6) for n in range(2)]


def dot(a, b):
    return jnp.dot(a, b, preferred_element_type=F32)


def dot_t(a, b):
    return lax.dot_general(a, b, (((1,), (1,)), ((), ())), preferred_element_type=F32)


def modulate(v, shift, scale):
    mean = jnp.mean(v, axis=-1, keepdims=True)
    cen = v - mean
    var = jnp.mean(cen * cen, axis=-1, keepdims=True)
    return (cen * lax.rsqrt(var + EPSILON) * (1.0 + scale) + shift).astype(BF16)


def grid(rows, cols):
    return (
        lax.broadcasted_iota(jnp.int32, (rows, cols), 0),
        lax.broadcasted_iota(jnp.int32, (rows, cols), 1),
    )


def flags(condition):
    return jnp.where(condition, 1.0, 0.0).astype(BF16)


def lane_masks(width, start):
    lane = lax.broadcasted_iota(jnp.int32, (1, width), 1)
    return [
        jnp.where((lane >= start + HEAD_DIM * h) & (lane < start + HEAD_DIM * (h + 1)), 1.0, 0.0)
        for h in range(HEADS)
    ]


def stack_heads(q, masks):
    return jnp.concatenate([(q * m).astype(BF16) for m in masks], axis=0)


def pick_heads(o, masks):
    n = o.shape[0] // HEADS
    total = o[0:n] * masks[0]
    for h in range(1, HEADS):
        total = total + o[h * n : (h + 1) * n] * masks[h]
    return total[:, PART:].astype(BF16)


def softmax(s):
    top = jnp.max(s, axis=-1, keepdims=True)
    e = jnp.exp(s - top)
    return (e / jnp.sum(e, axis=-1, keepdims=True)).astype(BF16)


def pack_part(v):
    rest = jnp.concatenate([v[32 * k : 32 * k + 32, 256:] for k in range(4)], axis=1)
    return jnp.concatenate([v[:, :128], v[:, 128:256], rest], axis=0)


def unpack_part(v):
    rest = jnp.concatenate([v[256:, 32 * k : 32 * k + 32] for k in range(4)], axis=0)
    return jnp.concatenate([v[:128], v[128:256], rest], axis=1)


def pack_kv(v):
    rest = jnp.concatenate([v[:64, 512:], v[64:, 512:]], axis=1)
    return jnp.concatenate([v[:, 128 * j : 128 * j + 128] for j in range(4)] + [rest], axis=0)


def unpack_kv(v):
    rest = jnp.concatenate([v[512:, :64], v[512:, 64:]], axis=0)
    return jnp.concatenate([v[128 * j : 128 * j + 128] for j in range(4)] + [rest], axis=1)


def kernel(
    lat, mod_h, wqkv_h, wo_h, tqkv_h, to_h, up_h, dn_h, o_ref,
    mod, w_s, w_so, w_t, w_to, w_up, w_dn, w_dp, c_s, c_t,
    lv, lp, g, lfull, qb, kvf, hp, halo, ps, r4, lsel, pk, a2, blk, pt, r7, blk2, pmp, r8, fin,
    spread_sel, unpack_sel, turn,
    wsem, s1, d1, sh, dh, s4, d4, s5, d5, s6, d6, s7, d7, s7b, d7b, s8, d8, s9, d9, zsem, ysem, xsem, csem,
):
    tm = lax.axis_index("tm")
    he = lax.axis_index("height")
    x = lax.axis_index("head")
    zlo, c = tm // 2, tm % 2
    zhi, y = he // 4, he % 4
    m_me = 4 * y + zlo
    f_me = 4 * zlo + y
    at_home = y // 2 == c
    away = y // 2 != c
    cross = zhi != c
    row_a, row_b = 1 - c, c
    row_of = (jnp.where(cross, row_a, row_b), jnp.where(cross, row_b, row_a))
    halo_of = (jnp.where(cross, 0, 1), jnp.where(cross, 1, 0))

    def dev(zlo, c, zhi, y, x):
        return (zlo * 2 + c, zhi * 4 + y, x)

    def xdev(k):
        return (tm, he, (x + k) % 4)

    def group_dev(m):
        return dev(m % 4, c, zhi, m // 4, x)

    def remote(src, dst, ssem, rsem, device):
        return pltpu.make_async_remote_copy(
            src_ref=src, dst_ref=dst, send_sem=ssem, recv_sem=rsem, device_id=device, device_id_type=MESH
        )

    def arrived(dst, rsem):
        pltpu.make_async_copy(dst, dst, rsem).wait()

    sent = []

    def send(copy):
        copy.start()
        sent.append(copy.wait_send)

    def send_if(condition, copy):
        pl.when(condition)(copy.start)
        sent.append(lambda: pl.when(condition)(copy.wait_send))

    loads = [
        pltpu.make_async_copy(wqkv_h, w_s, wsem.at[0]),
        pltpu.make_async_copy(wo_h, w_so, wsem.at[1]),
        pltpu.make_async_copy(tqkv_h, w_t, wsem.at[2]),
        pltpu.make_async_copy(to_h, w_to, wsem.at[3]),
        pltpu.make_async_copy(up_h, w_up, wsem.at[4]),
        pltpu.make_async_copy(dn_h, w_dn, wsem.at[5]),
        pltpu.make_async_copy(mod_h, mod, wsem.at[6]),
        pltpu.make_async_copy(lat, lv, wsem.at[7]),
    ]
    loads[7].start()

    bar = pltpu.get_barrier_semaphore()

    def tell(device):
        pl.semaphore_signal(bar, inc=1, device_id=device, device_id_type=MESH)

    def first_peer(i, k):
        return dev(zlo, y // 2, zhi, 2 * c + i, (x + k) % 4)

    z_near = zlo + 1 - 2 * (zlo % 2)
    z_far = (3 - zlo, (zlo + 2) % 4, z_near, zlo)

    def z_dev(z):
        return dev(z, c, zhi, y, x)

    for k in range(1, 4):
        for i in range(2):
            tell(first_peer(i, k))
    for k in range(1, 4):
        tell(xdev(k))
        tell(dev(zlo, c, zhi, (y + k) % 4, x))
    tell(dev(zlo, 1 - c, zhi, y, x))

    for k in range(1, 4):
        pl.when(zlo + k < 4)(lambda k=k: tell(z_dev(zlo + k)))
    cross_dev = dev(zlo, 1 - c, 1 - zhi, y, x)
    pl.when(cross & (zhi == 0))(lambda: tell(cross_dev))

    @pl.when(away)
    def _():
        for i in range(2):
            tell(first_peer(i, 0))

    for k in (6, 0, 5, 2, 1, 3, 4):
        loads[k].start()

    loads[7].wait()
    for i in range(2):
        lp[i] = pack_part(lv[i].astype(F32)).astype(BF16)
    pl.semaphore_wait(bar, 13 + zlo + jnp.where(cross & (zhi == 1), 1, 0) + jnp.where(away, 2, 0))

    slot = y % 2

    def first_copy(i, k):
        return remote(lp.at[i], g.at[x, slot], s1.at[i * 4 + k], d1.at[x * 2 + slot], first_peer(i, k))

    for k in (1, 3, 2):
        for i in range(2):
            send(first_copy(i, k))

    @pl.when(at_home)
    def _():
        pltpu.make_async_copy(lp.at[slot], g.at[x, slot], d1.at[x * 2 + slot]).start()

    send_if(at_home, first_copy(1 - slot, 0))
    for i in range(2):
        send_if(away, first_copy(i, 0))

    def answer(semaphore, device):
        pl.semaphore_signal(semaphore, inc=1, device_id=device, device_id_type=MESH)

    for k in range(1, 4):
        pl.when(zlo >= k)(lambda k=k: answer(zsem, z_dev(zlo - k)))
    pl.when(cross & (zhi == 1))(lambda: answer(xsem, cross_dev))

    q_masks = lane_masks(PART, 0)
    v_masks = lane_masks(2 * PART, PART)
    r, s = grid(256, 160)
    spread_sel[...] = flags((r // 16 == (s % 32) // 2) & ((r % 16) // 2 == s // 32) & (r % 2 == s % 2))
    r, s = grid(160, 256)
    unpack_sel[...] = flags((r % 16 == s // 16) & (r // 32 == (s % 16) // 2) & ((r % 32) // 16 == s % 2))
    r, s = grid(128, 128)
    order = flags(s == 8 * ((r % 32) // 2) + 2 * (r // 32) + r % 2)
    if CUT == 1:
        turn[...] = flags(s == 32 * ((r % 8) // 2) + 16 * (r % 2) + r // 8)
    else:
        turn[...] = flags(s == 64 * (r % 2) + 16 * ((r % 8) // 2) + r // 8)
    r, s = grid(32, 128)
    chosen = flags(s == 8 * (r // 2) + 2 * x + r % 2)

    @pl.when(jnp.logical_not(cross))
    def _():
        halo[1] = jnp.zeros((2 * PART, 128), BF16)

    loads[5].wait()

    def reorder(i, _):
        span = pl.ds(pl.multiple_of(i * 128, 128), 128)
        v = w_dn[span, :].astype(F32)
        pieces = [v[:, PART * k : PART * k + 256] for k in range(4)]
        pieces += [v[:, PART * k + 256 : PART * k + PART] for k in range(4)]
        w_dp[span, :] = jnp.concatenate(pieces, axis=1).astype(BF16)
        return 0

    lax.fori_loop(0, 9, reorder, 0)
    loads[6].wait()

    def turn_over(source, target):
        def step(i, _):
            span = pl.ds(pl.multiple_of(i * 128, 128), 128)
            v = source[:, span].astype(F32)
            v = jnp.concatenate([v[PART:], v[:PART]], axis=0)
            target[span, :] = v.T.astype(BF16)
            return 0

        lax.fori_loop(0, 9, step, 0)

    loads[0].wait()
    turn_over(w_s, c_s)
    loads[2].wait()
    turn_over(w_t, c_t)

    def prepare(t):
        for xs in range(4):
            arrived(g.at[xs, t], d1.at[xs * 2 + t])
        whole = jnp.concatenate([unpack_part(g[xs, t].astype(F32)) for xs in range(4)], axis=1)
        lfull[t] = whole.astype(BF16)
        normed = modulate(whole, mod[0:1], mod[1:2])
        kv = dot(normed, c_s[:, : 2 * PART])
        kvf[t] = kv.astype(BF16)
        hp[t] = pack_kv(kv).astype(BF16)
        return normed

    first, second = row_of[1], row_of[0]
    normed_first = prepare(first)
    pl.when(cross & (zhi == 0))(lambda: pl.semaphore_wait(xsem, 1))
    outer = remote(hp.at[row_b], halo.at[1], sh.at[1], dh.at[1], cross_dev)
    inner = remote(hp.at[row_a], halo.at[0], sh.at[0], dh.at[0], dev(zlo, 1 - c, zhi, y, x))
    send_if(cross, outer)
    send_if(jnp.logical_not(cross), inner)
    normed_second = prepare(second)
    send_if(cross, inner)
    for t, normed in ((second, normed_second), (first, normed_first)):
        qb[t] = dot(order, dot(normed, c_s[:, 2 * PART :]).astype(BF16)).astype(BF16)
    loads[1].wait()

    def spatial(n, bias):
        q4 = stack_heads(qb[row_of[n]].astype(F32), q_masks)
        kv = kvf[...].reshape(256, 2 * PART)
        far = unpack_kv(halo[halo_of[n]].astype(F32)).astype(BF16)
        s_own = dot_t(q4, kv[:, :PART]) * SCALE
        s_far = dot_t(q4, far[:, :PART]) * SCALE + bias
        p = softmax(jnp.concatenate([s_own, s_far], axis=1))
        o = pick_heads(dot(p[:, :256], kv) + dot(p[:, 256:], far), v_masks)
        ps[n] = dot(o, w_so[...]).astype(BF16)
        for k in (2, 1, 3):
            send(remote(
                ps.at[n, pl.ds(((x + k) % 4) * 32, 32)], r4.at[n, x], s4.at[n * 4 + k], d4.at[n * 4 + x], xdev(k)
            ))

    pl.when(zlo < 3)(lambda: pl.semaphore_wait(zsem, 3 - zlo))
    for k in range(1, 4):
        pl.when(zlo + k < 4)(lambda k=k: answer(ysem, z_dev(zlo + k)))
    pl.when(cross)(lambda: arrived(halo.at[0], dh.at[0]))
    spatial(0, jnp.where(cross, 0.0, -1e30))
    for n in range(2):
        lsel[n] = dot(chosen, lfull[row_of[n]]).astype(BF16)

    pl.when(cross)(lambda: arrived(halo.at[1], dh.at[1]))
    pl.when(jnp.logical_not(cross))(lambda: arrived(halo.at[0], dh.at[0]))
    spatial(1, 0.0)
    pl.when(zlo > 0)(lambda: pl.semaphore_wait(ysem, zlo))

    def gather(buf, i, ssem, rsem):
        for k in (2, 1, 3):
            send(remote(buf.at[i, x], buf.at[i, x], ssem.at[i * 4 + k], rsem.at[i * 4 + x], xdev(k)))

    def others(buf, i, rsem):
        for k in (1, 3, 2):
            xs = (x + k) % 4
            arrived(buf.at[i, xs], rsem.at[i * 4 + xs])

    def summed(mine, buf, i, rsem):
        total = mine.astype(F32)
        for k in (1, 3, 2):
            xs = (x + k) % 4
            arrived(buf.at[i, xs], rsem.at[i * 4 + xs])
            total = total + buf[i, xs].astype(F32)
        return total

    def stage_spread(n, u):
        total = summed(ps[n, pl.ds(x * 32, 32)], r4, n, d4)
        rows = (lsel[n].astype(F32) + mod[2:3] * total).astype(BF16)
        rows = jnp.concatenate([rows, jnp.zeros((32, 128), BF16)], axis=1)
        tall = jnp.concatenate([rows[:, 256 * j : 256 * j + 256] for j in range(5)], axis=0)
        pk[n] = dot(spread_sel[...], tall).astype(BF16).reshape(16, 16, 256)
        for j in range(4):
            for k in (2, 1, 3, 0):
                if j < 3 or k:
                    m = 4 * ((y + k) % 4) + z_far[j]
                    send(remote(
                        pk.at[n, m], a2.at[n, f_me], s5.at[n * 16 + 4 * j + k], d5.at[n * 16 + f_me], group_dev(m)
                    ))
        a2[n, f_me] = pk[n, m_me]

    def stage_gather(n, u):
        for k in range(1, 16):
            f = (f_me + k) % 16
            arrived(a2.at[n, f], d5.at[n * 16 + f])
        tall = dot(unpack_sel[...], a2[n].reshape(256, 256)).astype(BF16)
        wide = jnp.concatenate([tall[32 * j : 32 * j + 32] for j in range(5)], axis=1)
        for v in range(CUT):
            blk[n * CUT + v, x] = wide[v * RUN : (v + 1) * RUN, :D]
            gather(blk, n * CUT + v, s6, d6)

    def stage_temporal(n, u):
        i = n * CUT + u
        others(blk, i, d6)
        normed = modulate(blk[i].reshape(4 * RUN, D).astype(F32), mod[3:4], mod[4:5])
        qkv = dot(normed, c_t[...])
        q4 = stack_heads(qkv[:, 2 * PART :].astype(BF16).astype(F32), q_masks)
        kv = qkv[:, : 2 * PART].astype(BF16)
        r, s = grid(16 * RUN, 4 * RUN)
        sc = jnp.where((r % (4 * RUN)) // 16 == s // 16, dot_t(q4, kv[:, :PART]) * SCALE, -1e30)
        o = pick_heads(dot(softmax(sc), kv), v_masks)
        pt[i] = dot(o, w_to[...]).astype(BF16).reshape(4, RUN, D)
        for k in (2, 1, 3):
            send(remote(pt.at[i, (x + k) % 4], r7.at[i, x], s7.at[i * 4 + k], d7.at[i * 4 + x], xdev(k)))

    def stage_second(n, u):
        i = n * CUT + u
        total = summed(pt[i, x], r7, i, d7)
        blk2[i, x] = (blk[i, x].astype(F32) + mod[5:6] * total).astype(BF16)
        gather(blk2, i, s7b, d7b)

    def stage_mlp(n, u):
        for v in range(CUT):
            others(blk2, n * CUT + v, d7b)
        normed = modulate(blk2[n * CUT : (n + 1) * CUT].reshape(128, D).astype(F32), mod[6:7], mod[7:8])
        hidden = jax.nn.gelu(dot(normed, w_up[...]), approximate=True).astype(BF16)
        out = dot(hidden, w_dp[...])
        for xd in range(4):
            rest = [out[32 * k : 32 * k + 32, 1024 + 32 * xd : 1056 + 32 * xd] for k in range(4)]
            pmp[n, xd] = jnp.concatenate(
                [out[:, 256 * xd : 256 * xd + 128], out[:, 256 * xd + 128 : 256 * xd + 256],
                 jnp.concatenate(rest, axis=1)], axis=0,
            ).astype(BF16)
        for k in (2, 1, 3):
            send(remote(pmp.at[n, (x + k) % 4], r8.at[n, x], s8.at[n * 4 + k], d8.at[n * 4 + x], xdev(k)))

    def stage_return(n, u):
        lanes = pl.ds(pl.multiple_of(x * 256, 128), COVER)
        shift = (COVER - 32 * x) % COVER
        gate = pltpu.roll(jnp.broadcast_to(mod[8:9, lanes], (8, COVER)), shift, 1)[:1, :PART]
        base = pltpu.roll(blk2[n * CUT : (n + 1) * CUT, :, :, lanes].reshape(128, COVER).astype(F32), shift, 1)[:, :PART]
        total = unpack_part(summed(pmp[n, x], r8, n, d8))
        out = (base + gate * total).astype(BF16)
        fin[n] = dot(turn[...], out).astype(BF16).reshape(8, 16, PART)
        y_to = 2 * c + row_of[n]

        def back(j, kc):
            zd, cd = z_far[j], (c + kc) % 2
            return remote(
                fin.at[n, 2 * zd + cd], o_ref.at[m_me], s9.at[n * 8 + j * 2 + kc], d9.at[m_me], dev(zd, cd, zhi, y_to, x)
            )

        for j in range(4):
            for kc in range(2):
                if j < 3 or kc:
                    send(back(j, kc))
        here = y_to == y
        send_if(jnp.logical_not(here), back(3, 0))

        @pl.when(here)
        def _():
            pltpu.make_async_copy(fin.at[n, 2 * zlo + c], o_ref.at[m_me], d9.at[m_me]).start()

    for k in (3, 4):
        loads[k].wait()
    stages = (stage_spread, stage_gather, stage_temporal, stage_second, stage_mlp, stage_return)
    for k, n, u in ORDER:
        stages[k](n, u)
        if (k, n) == (1, 1):
            pl.semaphore_signal(csem, inc=1, device_id=dev(zlo, 1 - c, zhi, y, x), device_id_type=MESH)
        if (k, n) == (4, 0):
            pl.semaphore_wait(csem, 1)

    for done in sent:
        done()
    for m in range(16):
        arrived(o_ref.at[m], d9.at[m])


def body(latents, modulation, spatial_qkv, spatial_out, temporal_qkv, temporal_out, mlp_up, mlp_down):
    anywhere = pl.BlockSpec(memory_space=pl.ANY)
    sem = pltpu.SemaphoreType.DMA

    def vm(*shape):
        return pltpu.VMEM(shape, BF16)

    out = pl.pallas_call(
        kernel,
        out_shape=pltpu.VMEM((16, 16, PART), BF16),
        in_specs=[anywhere] * 8,
        out_specs=anywhere,
        scratch_shapes=[
            pltpu.VMEM((9, D), F32),
            vm(3 * PART, D), vm(PART, D), vm(3 * PART, D), vm(PART, D), vm(D, D), vm(D, D), vm(D, D),
            vm(D, 3 * PART), vm(D, 3 * PART),
            vm(2, 128, PART),
            vm(2, PART, 128),
            vm(4, 2, PART, 128),
            vm(2, 128, D),
            vm(2, 128, PART),
            vm(2, 128, 2 * PART),
            vm(2, 2 * PART, 128),
            vm(2, 2 * PART, 128),
            vm(2, 128, D),
            vm(2, 4, 32, D),
            vm(2, 32, D),
            vm(2, 16, 16, 256),
            vm(2, 16, 16, 256),
            vm(2 * CUT, 4, RUN, D),
            vm(2 * CUT, 4, RUN, D),
            vm(2 * CUT, 4, RUN, D),
            vm(2 * CUT, 4, RUN, D),
            vm(2, 4, PART, 128),
            vm(2, 4, PART, 128),
            vm(2, 8, 16, PART),
            vm(256, 160), vm(160, 256), vm(128, 128),
            sem((8,)),
            sem((8,)), sem((8,)), sem((2,)), sem((2,)), sem((8,)), sem((8,)), sem((32,)), sem((32,)),
            sem((8 * CUT,)), sem((8 * CUT,)), sem((8 * CUT,)), sem((8 * CUT,)), sem((8 * CUT,)), sem((8 * CUT,)),
            sem((8,)), sem((8,)), sem((16,)), sem((16,)),
            pltpu.SemaphoreType.REGULAR, pltpu.SemaphoreType.REGULAR,
            pltpu.SemaphoreType.REGULAR, pltpu.SemaphoreType.REGULAR,
        ],
        compiler_params=pltpu.CompilerParams(
            collective_id=0, has_side_effects=True, vmem_limit_bytes=60 * 2**20
        ),
        name="block",
    )(
        latents.reshape(2, 128, PART), modulation,
        jnp.swapaxes(spatial_qkv, 1, 2).reshape(3 * PART, D), spatial_out,
        jnp.swapaxes(temporal_qkv, 1, 2).reshape(3 * PART, D), temporal_out, mlp_up, mlp_down,
    )
    return out.reshape(16, 2, 8, PART).transpose(1, 0, 2, 3).reshape(latents.shape)


def solution(mesh):
    return jax.shard_map(
        body,
        mesh=mesh,
        in_specs=(
            P("tm", "height", None, "head"),
            P(),
            P(None, None, "head"),
            P("head", None),
            P(None, None, "head"),
            P("head", None),
            P(None, "head"),
            P("head", None),
        ),
        out_specs=P("tm", "height", None, "head"),
        check_vma=False,
    )
```

```python
import jax
import jax.numpy as jnp
from jax import lax
from jax.experimental import pallas as pl
from jax.experimental.pallas import tpu as pltpu
from jax.sharding import PartitionSpec as P

D = 1152
HEAD_DIM = 72
PART = 288
COVER = 384
HEADS = 4
EPSILON = 1e-06
SCALE = HEAD_DIM ** (-0.5)
MESH = pl.DeviceIdType.MESH
F32 = jnp.float32
BF16 = jnp.bfloat16
CUT = 2
RUN = 32 // CUT
ORDER = [
    (0, 0, 0), (0, 1, 0), (1, 0, 0), (1, 1, 0),
    (2, 0, 0), (2, 0, 1), (2, 1, 0), (2, 1, 1),
    (3, 0, 0), (3, 0, 1), (3, 1, 0), (3, 1, 1),
    (4, 0, 0), (4, 1, 0), (5, 0, 0), (5, 1, 0),
]


def dot(a, b):
    return jnp.dot(a, b, preferred_element_type=F32)


def dot_t(a, b):
    return lax.dot_general(a, b, (((1,), (1,)), ((), ())), preferred_element_type=F32)


def modulate(v, shift, scale):
    mean = jnp.mean(v, axis=-1, keepdims=True)
    cen = v - mean
    var = jnp.mean(cen * cen, axis=-1, keepdims=True)
    return (cen * lax.rsqrt(var + EPSILON) * (1.0 + scale) + shift).astype(BF16)


def grid(rows, cols):
    return (
        lax.broadcasted_iota(jnp.int32, (rows, cols), 0),
        lax.broadcasted_iota(jnp.int32, (rows, cols), 1),
    )


def flags(condition):
    return jnp.where(condition, 1.0, 0.0).astype(BF16)


def lane_masks(width, start):
    lane = lax.broadcasted_iota(jnp.int32, (1, width), 1)
    return [
        jnp.where((lane >= start + HEAD_DIM * h) & (lane < start + HEAD_DIM * (h + 1)), 1.0, 0.0)
        for h in range(HEADS)
    ]


def stack_heads(q, masks):
    return jnp.concatenate([(q * m).astype(BF16) for m in masks], axis=0)


def pick_heads(o, masks):
    n = o.shape[0] // HEADS
    total = o[0:n] * masks[0]
    for h in range(1, HEADS):
        total = total + o[h * n : (h + 1) * n] * masks[h]
    return total[:, PART:].astype(BF16)


def softmax(s):
    top = jnp.max(s, axis=-1, keepdims=True)
    e = jnp.exp(s - top)
    return (e / jnp.sum(e, axis=-1, keepdims=True)).astype(BF16)


def pack_part(v):
    rest = jnp.concatenate([v[32 * k : 32 * k + 32, 256:] for k in range(4)], axis=1)
    return jnp.concatenate([v[:, :128], v[:, 128:256], rest], axis=0)


def unpack_part(v):
    rest = jnp.concatenate([v[256:, 32 * k : 32 * k + 32] for k in range(4)], axis=0)
    return jnp.concatenate([v[:128], v[128:256], rest], axis=1)


def pack_kv(v):
    rest = jnp.concatenate([v[:64, 512:], v[64:, 512:]], axis=1)
    return jnp.concatenate([v[:, 128 * j : 128 * j + 128] for j in range(4)] + [rest], axis=0)


def unpack_kv(v):
    rest = jnp.concatenate([v[512:, :64], v[512:, 64:]], axis=0)
    return jnp.concatenate([v[128 * j : 128 * j + 128] for j in range(4)] + [rest], axis=1)


def kernel(
    lat, mod_h, wqkv_h, wo_h, tqkv_h, to_h, up_h, dn_h, o_ref,
    mod, w_s, w_so, w_t, w_to, w_up, w_dn, w_dp, c_s, c_t,
    lv, lp, g, lfull, qb, kvf, hp, halo, ps, r4, lsel, pk, a2, blk, pt, r7, blk2, pmp, r8, fin,
    spread_sel, unpack_sel, turn,
    wsem, s1, d1, sh, dh, s4, d4, s5, d5, s6, d6, s7, d7, s7b, d7b, s8, d8, s9, d9, asem, zsem, ysem, xsem, csem,
):
    tm = lax.axis_index("tm")
    he = lax.axis_index("height")
    x = lax.axis_index("head")
    zlo, c = tm // 2, tm % 2
    zhi, y = he // 4, he % 4
    m_me = 4 * y + zlo
    f_me = 4 * zlo + y
    at_home = y // 2 == c
    away = y // 2 != c
    cross = zhi != c
    row_a, row_b = 1 - c, c
    row_of = (jnp.where(cross, row_a, row_b), jnp.where(cross, row_b, row_a))
    halo_of = (jnp.where(cross, 0, 1), jnp.where(cross, 1, 0))

    def dev(zlo, c, zhi, y, x):
        return (zlo * 2 + c, zhi * 4 + y, x)

    def xdev(k):
        return (tm, he, (x + k) % 4)

    def group_dev(m):
        return dev(m % 4, c, zhi, m // 4, x)

    def remote(src, dst, ssem, rsem, device):
        return pltpu.make_async_remote_copy(
            src_ref=src, dst_ref=dst, send_sem=ssem, recv_sem=rsem, device_id=device, device_id_type=MESH
        )

    def arrived(dst, rsem):
        pltpu.make_async_copy(dst, dst, rsem).wait()

    sent = []

    def send(copy):
        copy.start()
        sent.append(copy.wait_send)

    def send_if(condition, copy):
        pl.when(condition)(copy.start)
        sent.append(lambda: pl.when(condition)(copy.wait_send))

    loads = [
        pltpu.make_async_copy(wqkv_h, w_s, wsem.at[0]),
        pltpu.make_async_copy(wo_h, w_so, wsem.at[1]),
        pltpu.make_async_copy(tqkv_h, w_t, wsem.at[2]),
        pltpu.make_async_copy(to_h, w_to, wsem.at[3]),
        pltpu.make_async_copy(up_h, w_up, wsem.at[4]),
        pltpu.make_async_copy(dn_h, w_dn, wsem.at[5]),
        pltpu.make_async_copy(mod_h, mod, wsem.at[6]),
        pltpu.make_async_copy(lat, lv, wsem.at[7]),
    ]
    loads[7].start()

    bar = pltpu.get_barrier_semaphore()

    def tell(device):
        pl.semaphore_signal(bar, inc=1, device_id=device, device_id_type=MESH)

    def first_peer(i, k):
        return dev(zlo, y // 2, zhi, 2 * c + i, (x + k) % 4)

    z_near = zlo + 1 - 2 * (zlo % 2)
    z_far = (3 - zlo, (zlo + 2) % 4, z_near, zlo)

    def z_dev(z):
        return dev(z, c, zhi, y, x)

    for k in range(1, 4):
        for i in range(2):
            tell(first_peer(i, k))
    for k in range(1, 4):
        pl.when(x + k < 4)(lambda k=k: tell(dev(zlo, c, zhi, y, x + k)))
        pl.when(y + k < 4)(lambda k=k: tell(dev(zlo, c, zhi, y + k, x)))
    core_dev = dev(zlo, 1 - c, zhi, y, x)
    pl.when(c == 0)(lambda: tell(core_dev))

    for k in range(1, 4):
        pl.when(zlo + k < 4)(lambda k=k: tell(z_dev(zlo + k)))
    cross_dev = dev(zlo, 1 - c, 1 - zhi, y, x)
    pl.when(cross & (zhi == 0))(lambda: tell(cross_dev))

    @pl.when(away)
    def _():
        for i in range(2):
            tell(first_peer(i, 0))

    pl.when(at_home)(lambda: tell(first_peer(1 - y % 2, 0)))

    for k in (6, 0, 5, 2, 1, 3, 4):
        loads[k].start()

    loads[7].wait()
    for i in range(2):
        lp[i] = pack_part(lv[i].astype(F32)).astype(BF16)
    pl.semaphore_wait(bar, 6 + x + y + c + zlo + jnp.where(cross & (zhi == 1), 1, 0) + jnp.where(away, 2, 1))

    slot = y % 2

    def first_copy(i, k):
        return remote(lp.at[i], g.at[x, slot], s1.at[i * 4 + k], d1.at[x * 2 + slot], first_peer(i, k))

    for k in (1, 3, 2):
        for i in range(2):
            send(first_copy(i, k))

    @pl.when(at_home)
    def _():
        pltpu.make_async_copy(lp.at[slot], g.at[x, slot], d1.at[x * 2 + slot]).start()

    send_if(at_home, first_copy(1 - slot, 0))
    for i in range(2):
        send_if(away, first_copy(i, 0))

    def answer(semaphore, device):
        pl.semaphore_signal(semaphore, inc=1, device_id=device, device_id_type=MESH)

    for k in range(1, 4):
        pl.when(x >= k)(lambda k=k: answer(asem, dev(zlo, c, zhi, y, x - k)))
        pl.when(y >= k)(lambda k=k: answer(asem, dev(zlo, c, zhi, y - k, x)))
    pl.when(c == 1)(lambda: answer(asem, core_dev))
    pl.when(cross & (zhi == 1))(lambda: answer(xsem, cross_dev))

    q_masks = lane_masks(PART, 0)
    v_masks = lane_masks(2 * PART, PART)
    r, s = grid(256, 160)
    spread_sel[...] = flags((r // 16 == (s % 32) // 2) & ((r % 16) // 2 == s // 32) & (r % 2 == s % 2))
    r, s = grid(160, 256)
    unpack_sel[...] = flags((r % 16 == s // 16) & (r // 32 == (s % 16) // 2) & ((r % 32) // 16 == s % 2))
    r, s = grid(128, 128)
    order = flags(s == 8 * ((r % 32) // 2) + 2 * (r // 32) + r % 2)
    if CUT == 1:
        turn[...] = flags(s == 32 * ((r % 8) // 2) + 16 * (r % 2) + r // 8)
    else:
        turn[...] = flags(s == 64 * (r % 2) + 16 * ((r % 8) // 2) + r // 8)
    r, s = grid(32, 128)
    chosen = flags(s == 8 * (r // 2) + 2 * x + r % 2)

    @pl.when(jnp.logical_not(cross))
    def _():
        halo[1] = jnp.zeros((2 * PART, 128), BF16)

    loads[5].wait()

    def reorder(i, _):
        span = pl.ds(pl.multiple_of(i * 128, 128), 128)
        v = w_dn[span, :].astype(F32)
        pieces = [v[:, PART * k : PART * k + 256] for k in range(4)]
        pieces += [v[:, PART * k + 256 : PART * k + PART] for k in range(4)]
        w_dp[span, :] = jnp.concatenate(pieces, axis=1).astype(BF16)
        return 0

    lax.fori_loop(0, 9, reorder, 0)
    loads[6].wait()

    def turn_over(source, target):
        def step(i, _):
            span = pl.ds(pl.multiple_of(i * 128, 128), 128)
            v = source[:, span].astype(F32)
            v = jnp.concatenate([v[PART:], v[:PART]], axis=0)
            target[span, :] = v.T.astype(BF16)
            return 0

        lax.fori_loop(0, 9, step, 0)

    loads[0].wait()
    turn_over(w_s, c_s)
    loads[2].wait()
    turn_over(w_t, c_t)

    def prepare(t):
        for xs in range(4):
            arrived(g.at[xs, t], d1.at[xs * 2 + t])
        whole = jnp.concatenate([unpack_part(g[xs, t].astype(F32)) for xs in range(4)], axis=1)
        lfull[t] = whole.astype(BF16)
        normed = modulate(whole, mod[0:1], mod[1:2])
        kv = dot(normed, c_s[:, : 2 * PART])
        kvf[t] = kv.astype(BF16)
        hp[t] = pack_kv(kv).astype(BF16)
        return normed

    first, second = row_of[1], row_of[0]
    normed_first = prepare(first)
    waits = 7 - x - y - c
    pl.when(waits > 0)(lambda: pl.semaphore_wait(asem, waits))
    for k in range(1, 4):
        pl.when(zlo >= k)(lambda k=k: answer(zsem, z_dev(zlo - k)))
    pl.when(cross & (zhi == 0))(lambda: pl.semaphore_wait(xsem, 1))
    outer = remote(hp.at[row_b], halo.at[1], sh.at[1], dh.at[1], cross_dev)
    inner = remote(hp.at[row_a], halo.at[0], sh.at[0], dh.at[0], dev(zlo, 1 - c, zhi, y, x))
    send_if(cross, outer)
    send_if(jnp.logical_not(cross), inner)
    normed_second = prepare(second)
    send_if(cross, inner)
    for t, normed in ((second, normed_second), (first, normed_first)):
        qb[t] = dot(order, dot(normed, c_s[:, 2 * PART :]).astype(BF16)).astype(BF16)
    loads[1].wait()

    def spatial(n, bias):
        q4 = stack_heads(qb[row_of[n]].astype(F32), q_masks)
        kv = kvf[...].reshape(256, 2 * PART)
        far = unpack_kv(halo[halo_of[n]].astype(F32)).astype(BF16)
        s_own = dot_t(q4, kv[:, :PART]) * SCALE
        s_far = dot_t(q4, far[:, :PART]) * SCALE + bias
        p = softmax(jnp.concatenate([s_own, s_far], axis=1))
        o = pick_heads(dot(p[:, :256], kv) + dot(p[:, 256:], far), v_masks)
        ps[n] = dot(o, w_so[...]).astype(BF16)
        for k in (2, 1, 3):
            send(remote(
                ps.at[n, pl.ds(((x + k) % 4) * 32, 32)], r4.at[n, x], s4.at[n * 4 + k], d4.at[n * 4 + x], xdev(k)
            ))

    pl.when(cross)(lambda: arrived(halo.at[0], dh.at[0]))
    spatial(0, jnp.where(cross, 0.0, -1e30))
    for n in range(2):
        lsel[n] = dot(chosen, lfull[row_of[n]]).astype(BF16)

    pl.when(cross)(lambda: arrived(halo.at[1], dh.at[1]))
    pl.when(jnp.logical_not(cross))(lambda: arrived(halo.at[0], dh.at[0]))
    spatial(1, 0.0)
    pl.when(zlo < 3)(lambda: pl.semaphore_wait(zsem, 3 - zlo))
    for k in range(1, 4):
        pl.when(zlo + k < 4)(lambda k=k: answer(ysem, z_dev(zlo + k)))
    pl.when(zlo > 0)(lambda: pl.semaphore_wait(ysem, zlo))

    def gather(buf, i, ssem, rsem):
        for k in (2, 1, 3):
            send(remote(buf.at[i, x], buf.at[i, x], ssem.at[i * 4 + k], rsem.at[i * 4 + x], xdev(k)))

    def others(buf, i, rsem):
        for k in (1, 3, 2):
            xs = (x + k) % 4
            arrived(buf.at[i, xs], rsem.at[i * 4 + xs])

    def summed(mine, buf, i, rsem):
        total = mine.astype(F32)
        for k in (1, 3, 2):
            xs = (x + k) % 4
            arrived(buf.at[i, xs], rsem.at[i * 4 + xs])
            total = total + buf[i, xs].astype(F32)
        return total

    def stage_spread(n, u):
        total = summed(ps[n, pl.ds(x * 32, 32)], r4, n, d4)
        rows = (lsel[n].astype(F32) + mod[2:3] * total).astype(BF16)
        rows = jnp.concatenate([rows, jnp.zeros((32, 128), BF16)], axis=1)
        tall = jnp.concatenate([rows[:, 256 * j : 256 * j + 256] for j in range(5)], axis=0)
        pk[n] = dot(spread_sel[...], tall).astype(BF16).reshape(16, 16, 256)
        for j in range(4):
            for k in (2, 1, 3, 0):
                if j < 3 or k:
                    m = 4 * ((y + k) % 4) + z_far[j]
                    send(remote(
                        pk.at[n, m], a2.at[n, f_me], s5.at[n * 16 + 4 * j + k], d5.at[n * 16 + f_me], group_dev(m)
                    ))
        a2[n, f_me] = pk[n, m_me]

    def stage_gather(n, u):
        for k in range(1, 16):
            f = (f_me + k) % 16
            arrived(a2.at[n, f], d5.at[n * 16 + f])
        tall = dot(unpack_sel[...], a2[n].reshape(256, 256)).astype(BF16)
        wide = jnp.concatenate([tall[32 * j : 32 * j + 32] for j in range(5)], axis=1)
        for v in range(CUT):
            blk[n * CUT + v, x] = wide[v * RUN : (v + 1) * RUN, :D]
            gather(blk, n * CUT + v, s6, d6)

    def stage_temporal(n, u):
        i = n * CUT + u
        others(blk, i, d6)
        normed = modulate(blk[i].reshape(4 * RUN, D).astype(F32), mod[3:4], mod[4:5])
        qkv = dot(normed, c_t[...])
        q4 = stack_heads(qkv[:, 2 * PART :].astype(BF16).astype(F32), q_masks)
        kv = qkv[:, : 2 * PART].astype(BF16)
        r, s = grid(16 * RUN, 4 * RUN)
        sc = jnp.where((r % (4 * RUN)) // 16 == s // 16, dot_t(q4, kv[:, :PART]) * SCALE, -1e30)
        o = pick_heads(dot(softmax(sc), kv), v_masks)
        pt[i] = dot(o, w_to[...]).astype(BF16).reshape(4, RUN, D)
        for k in (2, 1, 3):
            send(remote(pt.at[i, (x + k) % 4], r7.at[i, x], s7.at[i * 4 + k], d7.at[i * 4 + x], xdev(k)))

    def stage_second(n, u):
        i = n * CUT + u
        total = summed(pt[i, x], r7, i, d7)
        blk2[i, x] = (blk[i, x].astype(F32) + mod[5:6] * total).astype(BF16)
        gather(blk2, i, s7b, d7b)

    def stage_mlp(n, u):
        for v in range(CUT):
            others(blk2, n * CUT + v, d7b)
        normed = modulate(blk2[n * CUT : (n + 1) * CUT].reshape(128, D).astype(F32), mod[6:7], mod[7:8])
        hidden = jax.nn.gelu(dot(normed, w_up[...]), approximate=True).astype(BF16)
        out = dot(hidden, w_dp[...])
        for xd in range(4):
            rest = [out[32 * k : 32 * k + 32, 1024 + 32 * xd : 1056 + 32 * xd] for k in range(4)]
            pmp[n, xd] = jnp.concatenate(
                [out[:, 256 * xd : 256 * xd + 128], out[:, 256 * xd + 128 : 256 * xd + 256],
                 jnp.concatenate(rest, axis=1)], axis=0,
            ).astype(BF16)
        for k in (2, 1, 3):
            send(remote(pmp.at[n, (x + k) % 4], r8.at[n, x], s8.at[n * 4 + k], d8.at[n * 4 + x], xdev(k)))

    def stage_return(n, u):
        lanes = pl.ds(pl.multiple_of(x * 256, 128), COVER)
        shift = (COVER - 32 * x) % COVER
        gate = pltpu.roll(jnp.broadcast_to(mod[8:9, lanes], (8, COVER)), shift, 1)[:1, :PART]
        base = pltpu.roll(blk2[n * CUT : (n + 1) * CUT, :, :, lanes].reshape(128, COVER).astype(F32), shift, 1)[:, :PART]
        total = unpack_part(summed(pmp[n, x], r8, n, d8))
        out = (base + gate * total).astype(BF16)
        fin[n] = dot(turn[...], out).astype(BF16).reshape(8, 16, PART)
        y_to = 2 * c + row_of[n]

        def back(j, kc):
            zd, cd = z_far[j], (c + kc) % 2
            return remote(
                fin.at[n, 2 * zd + cd], o_ref.at[m_me], s9.at[n * 8 + j * 2 + kc], d9.at[m_me], dev(zd, cd, zhi, y_to, x)
            )

        for j in range(4):
            for kc in range(2):
                if j < 3 or kc:
                    send(back(j, kc))
        here = y_to == y
        send_if(jnp.logical_not(here), back(3, 0))

        @pl.when(here)
        def _():
            pltpu.make_async_copy(fin.at[n, 2 * zlo + c], o_ref.at[m_me], d9.at[m_me]).start()

    for k in (3, 4):
        loads[k].wait()
    stages = (stage_spread, stage_gather, stage_temporal, stage_second, stage_mlp, stage_return)
    for k, n, u in ORDER:
        stages[k](n, u)
        if (k, n) == (1, 1):
            pl.semaphore_signal(csem, inc=1, device_id=dev(zlo, 1 - c, zhi, y, x), device_id_type=MESH)
        if (k, n) == (4, 0):
            pl.semaphore_wait(csem, 1)

    for done in sent:
        done()
    for m in range(16):
        arrived(o_ref.at[m], d9.at[m])


def body(latents, modulation, spatial_qkv, spatial_out, temporal_qkv, temporal_out, mlp_up, mlp_down):
    anywhere = pl.BlockSpec(memory_space=pl.ANY)
    sem = pltpu.SemaphoreType.DMA

    def vm(*shape):
        return pltpu.VMEM(shape, BF16)

    out = pl.pallas_call(
        kernel,
        out_shape=pltpu.VMEM((16, 16, PART), BF16),
        in_specs=[anywhere] * 8,
        out_specs=anywhere,
        scratch_shapes=[
            pltpu.VMEM((9, D), F32),
            vm(3 * PART, D), vm(PART, D), vm(3 * PART, D), vm(PART, D), vm(D, D), vm(D, D), vm(D, D),
            vm(D, 3 * PART), vm(D, 3 * PART),
            vm(2, 128, PART),
            vm(2, PART, 128),
            vm(4, 2, PART, 128),
            vm(2, 128, D),
            vm(2, 128, PART),
            vm(2, 128, 2 * PART),
            vm(2, 2 * PART, 128),
            vm(2, 2 * PART, 128),
            vm(2, 128, D),
            vm(2, 4, 32, D),
            vm(2, 32, D),
            vm(2, 16, 16, 256),
            vm(2, 16, 16, 256),
            vm(2 * CUT, 4, RUN, D),
            vm(2 * CUT, 4, RUN, D),
            vm(2 * CUT, 4, RUN, D),
            vm(2 * CUT, 4, RUN, D),
            vm(2, 4, PART, 128),
            vm(2, 4, PART, 128),
            vm(2, 8, 16, PART),
            vm(256, 160), vm(160, 256), vm(128, 128),
            sem((8,)),
            sem((8,)), sem((8,)), sem((2,)), sem((2,)), sem((8,)), sem((8,)), sem((32,)), sem((32,)),
            sem((8 * CUT,)), sem((8 * CUT,)), sem((8 * CUT,)), sem((8 * CUT,)), sem((8 * CUT,)), sem((8 * CUT,)),
            sem((8,)), sem((8,)), sem((16,)), sem((16,)),
            pltpu.SemaphoreType.REGULAR, pltpu.SemaphoreType.REGULAR, pltpu.SemaphoreType.REGULAR,
            pltpu.SemaphoreType.REGULAR, pltpu.SemaphoreType.REGULAR,
        ],
        compiler_params=pltpu.CompilerParams(
            collective_id=0, has_side_effects=True, vmem_limit_bytes=60 * 2**20
        ),
        name="block",
    )(
        latents.reshape(2, 128, PART), modulation,
        jnp.swapaxes(spatial_qkv, 1, 2).reshape(3 * PART, D), spatial_out,
        jnp.swapaxes(temporal_qkv, 1, 2).reshape(3 * PART, D), temporal_out, mlp_up, mlp_down,
    )
    return out.reshape(16, 2, 8, PART).transpose(1, 0, 2, 3).reshape(latents.shape)


def solution(mesh):
    return jax.shard_map(
        body,
        mesh=mesh,
        in_specs=(
            P("tm", "height", None, "head"),
            P(),
            P(None, None, "head"),
            P("head", None),
            P(None, None, "head"),
            P("head", None),
            P(None, "head"),
            P("head", None),
        ),
        out_specs=P("tm", "height", None, "head"),
        check_vma=False,
    )
```

```python
import jax
import jax.numpy as jnp
from jax import lax
from jax.experimental import pallas as pl
from jax.experimental.pallas import tpu as pltpu
from jax.sharding import PartitionSpec as P

D = 1152
HEAD_DIM = 72
PART = 288
COVER = 384
HEADS = 4
EPSILON = 1e-06
SCALE = HEAD_DIM ** (-0.5)
MESH = pl.DeviceIdType.MESH
F32 = jnp.float32
BF16 = jnp.bfloat16
CUT = 2
RUN = 32 // CUT
ORDER = [
    (0, 0, 0), (0, 1, 0), (1, 0, 0), (1, 1, 0),
    (2, 0, 0), (2, 0, 1), (2, 1, 0), (2, 1, 1),
    (3, 0, 0), (3, 0, 1), (3, 1, 0), (3, 1, 1),
    (4, 0, 0), (4, 1, 0), (5, 0, 0), (5, 1, 0),
]


def dot(a, b):
    return jnp.dot(a, b, preferred_element_type=F32)


def dot_t(a, b):
    return lax.dot_general(a, b, (((1,), (1,)), ((), ())), preferred_element_type=F32)


def modulate(v, shift, scale):
    mean = jnp.mean(v, axis=-1, keepdims=True)
    cen = v - mean
    var = jnp.mean(cen * cen, axis=-1, keepdims=True)
    return (cen * lax.rsqrt(var + EPSILON) * (1.0 + scale) + shift).astype(BF16)


def grid(rows, cols):
    return (
        lax.broadcasted_iota(jnp.int32, (rows, cols), 0),
        lax.broadcasted_iota(jnp.int32, (rows, cols), 1),
    )


def flags(condition):
    return jnp.where(condition, 1.0, 0.0).astype(BF16)


def lane_masks(width, start):
    lane = lax.broadcasted_iota(jnp.int32, (1, width), 1)
    return [
        jnp.where((lane >= start + HEAD_DIM * h) & (lane < start + HEAD_DIM * (h + 1)), 1.0, 0.0)
        for h in range(HEADS)
    ]


def stack_heads(q, masks):
    return jnp.concatenate([(q * m).astype(BF16) for m in masks], axis=0)


def pick_heads(o, masks):
    n = o.shape[0] // HEADS
    total = o[0:n] * masks[0]
    for h in range(1, HEADS):
        total = total + o[h * n : (h + 1) * n] * masks[h]
    return total[:, PART:].astype(BF16)


def softmax(s):
    top = jnp.max(s, axis=-1, keepdims=True)
    e = jnp.exp(s - top)
    return (e / jnp.sum(e, axis=-1, keepdims=True)).astype(BF16)


def pack_part(v):
    rest = jnp.concatenate([v[32 * k : 32 * k + 32, 256:] for k in range(4)], axis=1)
    return jnp.concatenate([v[:, :128], v[:, 128:256], rest], axis=0)


def unpack_part(v):
    rest = jnp.concatenate([v[256:, 32 * k : 32 * k + 32] for k in range(4)], axis=0)
    return jnp.concatenate([v[:128], v[128:256], rest], axis=1)


def pack_kv(v):
    rest = jnp.concatenate([v[:64, 512:], v[64:, 512:]], axis=1)
    return jnp.concatenate([v[:, 128 * j : 128 * j + 128] for j in range(4)] + [rest], axis=0)


def unpack_kv(v):
    rest = jnp.concatenate([v[512:, :64], v[512:, 64:]], axis=0)
    return jnp.concatenate([v[128 * j : 128 * j + 128] for j in range(4)] + [rest], axis=1)


def kernel(
    lat, mod_h, wqkv_h, wo_h, tqkv_h, to_h, up_h, dn_h, o_ref,
    mod, w_s, w_so, w_t, w_to, w_up, w_dn, w_dp, c_s, c_t,
    lv, lp, g, lfull, qb, kvf, hp, halo, ps, r4, lsel, pk, a2, blk, pt, r7, blk2, pmp, r8, fin,
    spread_sel, unpack_sel, turn,
    wsem, s1, d1, sh, dh, s4, d4, s5, d5, s6, d6, s7, d7, s7b, d7b, s8, d8, s9, d9, asem, zsem, ysem, xsem, csem,
):
    tm = lax.axis_index("tm")
    he = lax.axis_index("height")
    x = lax.axis_index("head")
    zlo, c = tm // 2, tm % 2
    zhi, y = he // 4, he % 4
    m_me = 4 * y + zlo
    f_me = 4 * zlo + y
    at_home = y // 2 == c
    away = y // 2 != c
    cross = zhi != c
    row_a, row_b = 1 - c, c
    row_of = (jnp.where(cross, row_a, row_b), jnp.where(cross, row_b, row_a))
    halo_of = (jnp.where(cross, 0, 1), jnp.where(cross, 1, 0))

    def dev(zlo, c, zhi, y, x):
        return (zlo * 2 + c, zhi * 4 + y, x)

    def xdev(k):
        return (tm, he, (x + k) % 4)

    def group_dev(m):
        return dev(m % 4, c, zhi, m // 4, x)

    def remote(src, dst, ssem, rsem, device):
        return pltpu.make_async_remote_copy(
            src_ref=src, dst_ref=dst, send_sem=ssem, recv_sem=rsem, device_id=device, device_id_type=MESH
        )

    def arrived(dst, rsem):
        pltpu.make_async_copy(dst, dst, rsem).wait()

    sent = []

    def send(copy):
        copy.start()
        sent.append(copy.wait_send)

    def send_if(condition, copy):
        pl.when(condition)(copy.start)
        sent.append(lambda: pl.when(condition)(copy.wait_send))

    loads = [
        pltpu.make_async_copy(wqkv_h, w_s, wsem.at[0]),
        pltpu.make_async_copy(wo_h, w_so, wsem.at[1]),
        pltpu.make_async_copy(tqkv_h, w_t, wsem.at[2]),
        pltpu.make_async_copy(to_h, w_to, wsem.at[3]),
        pltpu.make_async_copy(up_h, w_up, wsem.at[4]),
        pltpu.make_async_copy(dn_h, w_dn, wsem.at[5]),
        pltpu.make_async_copy(mod_h, mod, wsem.at[6]),
        pltpu.make_async_copy(lat, lv, wsem.at[7]),
    ]
    loads[7].start()

    bar = pltpu.get_barrier_semaphore()

    def tell(device):
        pl.semaphore_signal(bar, inc=1, device_id=device, device_id_type=MESH)

    def first_peer(i, k):
        return dev(zlo, y // 2, zhi, 2 * c + i, (x + k) % 4)

    z_near = zlo + 1 - 2 * (zlo % 2)
    z_far = (3 - zlo, (zlo + 2) % 4, z_near, zlo)

    def z_dev(z):
        return dev(z, c, zhi, y, x)

    for k in range(1, 4):
        for i in range(2):
            tell(first_peer(i, k))
    for k in range(1, 4):
        pl.when(x + k < 4)(lambda k=k: tell(dev(zlo, c, zhi, y, x + k)))
        pl.when(y + k < 4)(lambda k=k: tell(dev(zlo, c, zhi, y + k, x)))
    core_dev = dev(zlo, 1 - c, zhi, y, x)
    pl.when(c == 0)(lambda: tell(core_dev))

    for k in range(1, 4):
        pl.when(zlo + k < 4)(lambda k=k: tell(z_dev(zlo + k)))
    cross_dev = dev(zlo, 1 - c, 1 - zhi, y, x)
    pl.when(cross & (zhi == 0))(lambda: tell(cross_dev))

    @pl.when(away)
    def _():
        for i in range(2):
            tell(first_peer(i, 0))

    pl.when(at_home)(lambda: tell(first_peer(1 - y % 2, 0)))

    for k in (6, 0, 5, 2, 1, 3, 4):
        loads[k].start()

    loads[7].wait()
    for i in range(2):
        lp[i] = pack_part(lv[i].astype(F32)).astype(BF16)
    pl.semaphore_wait(bar, 6 + x + y + c + zlo + jnp.where(cross & (zhi == 1), 1, 0) + jnp.where(away, 2, 1))

    slot = y % 2

    def first_copy(i, k):
        return remote(lp.at[i], g.at[x, slot], s1.at[i * 4 + k], d1.at[x * 2 + slot], first_peer(i, k))

    for k in (1, 3, 2):
        for i in range(2):
            send(first_copy(i, k))

    @pl.when(at_home)
    def _():
        pltpu.make_async_copy(lp.at[slot], g.at[x, slot], d1.at[x * 2 + slot]).start()

    send_if(at_home, first_copy(1 - slot, 0))
    for i in range(2):
        send_if(away, first_copy(i, 0))

    def answer(semaphore, device):
        pl.semaphore_signal(semaphore, inc=1, device_id=device, device_id_type=MESH)

    for k in range(1, 4):
        pl.when(x >= k)(lambda k=k: answer(asem, dev(zlo, c, zhi, y, x - k)))
        pl.when(y >= k)(lambda k=k: answer(asem, dev(zlo, c, zhi, y - k, x)))
    pl.when(c == 1)(lambda: answer(asem, core_dev))
    pl.when(cross & (zhi == 1))(lambda: answer(xsem, cross_dev))

    q_masks = lane_masks(PART, 0)
    v_masks = lane_masks(2 * PART, PART)
    r, s = grid(256, 160)
    spread_sel[...] = flags((r // 16 == (s % 32) // 2) & ((r % 16) // 2 == s // 32) & (r % 2 == s % 2))
    r, s = grid(160, 256)
    unpack_sel[...] = flags((r % 16 == s // 16) & (r // 32 == (s % 16) // 2) & ((r % 32) // 16 == s % 2))
    r, s = grid(128, 128)
    order = flags(s == 8 * ((r % 32) // 2) + 2 * (r // 32) + r % 2)
    if CUT == 1:
        turn[...] = flags(s == 32 * ((r % 8) // 2) + 16 * (r % 2) + r // 8)
    else:
        turn[...] = flags(s == 64 * (r % 2) + 16 * ((r % 8) // 2) + r // 8)
    r, s = grid(32, 128)
    chosen = flags(s == 8 * (r // 2) + 2 * x + r % 2)

    @pl.when(jnp.logical_not(cross))
    def _():
        halo[1] = jnp.zeros((2 * PART, 128), BF16)

    loads[5].wait()

    def reorder(i, _):
        span = pl.ds(pl.multiple_of(i * 128, 128), 128)
        v = w_dn[span, :].astype(F32)
        pieces = [v[:, PART * k : PART * k + 256] for k in range(4)]
        pieces += [v[:, PART * k + 256 : PART * k + PART] for k in range(4)]
        w_dp[span, :] = jnp.concatenate(pieces, axis=1).astype(BF16)
        return 0

    lax.fori_loop(0, 9, reorder, 0)
    loads[6].wait()

    def turn_over(source, target):
        def step(i, _):
            span = pl.ds(pl.multiple_of(i * 128, 128), 128)
            v = source[:, span].astype(F32)
            v = jnp.concatenate([v[PART:], v[:PART]], axis=0)
            target[span, :] = v.T.astype(BF16)
            return 0

        lax.fori_loop(0, 9, step, 0)

    loads[0].wait()
    turn_over(w_s, c_s)
    loads[2].wait()
    turn_over(w_t, c_t)

    def prepare(t):
        for xs in range(4):
            arrived(g.at[xs, t], d1.at[xs * 2 + t])
        whole = jnp.concatenate([unpack_part(g[xs, t].astype(F32)) for xs in range(4)], axis=1)
        lfull[t] = whole.astype(BF16)
        normed = modulate(whole, mod[0:1], mod[1:2])
        kv = dot(normed, c_s[:, : 2 * PART])
        kvf[t] = kv.astype(BF16)
        hp[t] = pack_kv(kv).astype(BF16)
        return normed

    first, second = row_of[1], row_of[0]
    normed_first = prepare(first)
    waits = 7 - x - y - c
    pl.when(waits > 0)(lambda: pl.semaphore_wait(asem, waits))
    for k in range(1, 4):
        pl.when(zlo >= k)(lambda k=k: answer(zsem, z_dev(zlo - k)))
    pl.when(cross & (zhi == 0))(lambda: pl.semaphore_wait(xsem, 1))
    outer = remote(hp.at[row_b], halo.at[1], sh.at[1], dh.at[1], cross_dev)
    inner = remote(hp.at[row_a], halo.at[0], sh.at[0], dh.at[0], dev(zlo, 1 - c, zhi, y, x))
    send_if(cross, outer)
    send_if(jnp.logical_not(cross), inner)
    normed_second = prepare(second)
    send_if(cross, inner)
    for t, normed in ((second, normed_second), (first, normed_first)):
        qb[t] = dot(order, dot(normed, c_s[:, 2 * PART :]).astype(BF16)).astype(BF16)
    loads[1].wait()

    def spatial(n, bias):
        q4 = stack_heads(qb[row_of[n]].astype(F32), q_masks)
        kv = kvf[...].reshape(256, 2 * PART)
        far = unpack_kv(halo[halo_of[n]].astype(F32)).astype(BF16)
        s_own = dot_t(q4, kv[:, :PART]) * SCALE
        s_far = dot_t(q4, far[:, :PART]) * SCALE + bias
        p = softmax(jnp.concatenate([s_own, s_far], axis=1))
        o = pick_heads(dot(p[:, :256], kv) + dot(p[:, 256:], far), v_masks)
        ps[n] = dot(o, w_so[...]).astype(BF16)
        for k in (2, 1, 3):
            send(remote(
                ps.at[n, pl.ds(((x + k) % 4) * 32, 32)], r4.at[n, x], s4.at[n * 4 + k], d4.at[n * 4 + x], xdev(k)
            ))

    pl.when(cross)(lambda: arrived(halo.at[0], dh.at[0]))
    spatial(0, jnp.where(cross, 0.0, -1e30))
    for n in range(2):
        lsel[n] = dot(chosen, lfull[row_of[n]]).astype(BF16)

    pl.when(cross)(lambda: arrived(halo.at[1], dh.at[1]))
    pl.when(jnp.logical_not(cross))(lambda: arrived(halo.at[0], dh.at[0]))
    spatial(1, 0.0)
    pl.when(zlo < 3)(lambda: pl.semaphore_wait(zsem, 3 - zlo))
    for k in range(1, 4):
        pl.when(zlo + k < 4)(lambda k=k: answer(ysem, z_dev(zlo + k)))
    pl.when(zlo > 0)(lambda: pl.semaphore_wait(ysem, zlo))

    def gather(buf, i, ssem, rsem):
        for k in (2, 1, 3):
            send(remote(buf.at[i, x], buf.at[i, x], ssem.at[i * 4 + k], rsem.at[i * 4 + x], xdev(k)))

    def others(buf, i, rsem):
        for k in (1, 3, 2):
            xs = (x + k) % 4
            arrived(buf.at[i, xs], rsem.at[i * 4 + xs])

    def summed(mine, buf, i, rsem):
        total = mine.astype(F32)
        for k in (1, 3, 2):
            xs = (x + k) % 4
            arrived(buf.at[i, xs], rsem.at[i * 4 + xs])
            total = total + buf[i, xs].astype(F32)
        return total

    def stage_spread(n, u):
        total = summed(ps[n, pl.ds(x * 32, 32)], r4, n, d4)
        rows = (lsel[n].astype(F32) + mod[2:3] * total).astype(BF16)
        rows = jnp.concatenate([rows, jnp.zeros((32, 128), BF16)], axis=1)
        tall = jnp.concatenate([rows[:, 256 * j : 256 * j + 256] for j in range(5)], axis=0)
        pk[n] = dot(spread_sel[...], tall).astype(BF16).reshape(16, 16, 256)
        for j in range(4):
            for k in (2, 1, 3, 0):
                if j < 3 or k:
                    m = 4 * ((y + k) % 4) + z_far[j]
                    send(remote(
                        pk.at[n, m], a2.at[n, f_me], s5.at[n * 16 + 4 * j + k], d5.at[n * 16 + f_me], group_dev(m)
                    ))
        a2[n, f_me] = pk[n, m_me]

    def stage_gather(n, u):
        for k in range(1, 16):
            f = (f_me + k) % 16
            arrived(a2.at[n, f], d5.at[n * 16 + f])
        tall = dot(unpack_sel[...], a2[n].reshape(256, 256)).astype(BF16)
        wide = jnp.concatenate([tall[32 * j : 32 * j + 32] for j in range(5)], axis=1)
        for v in range(CUT):
            blk[n * CUT + v, x] = wide[v * RUN : (v + 1) * RUN, :D]
            gather(blk, n * CUT + v, s6, d6)

    def stage_temporal(n, u):
        i = n * CUT + u
        others(blk, i, d6)
        normed = modulate(blk[i].reshape(4 * RUN, D).astype(F32), mod[3:4], mod[4:5])
        qkv = dot(normed, c_t[...])
        q4 = stack_heads(qkv[:, 2 * PART :].astype(BF16).astype(F32), q_masks)
        kv = qkv[:, : 2 * PART].astype(BF16)
        r, s = grid(16 * RUN, 4 * RUN)
        sc = jnp.where((r % (4 * RUN)) // 16 == s // 16, dot_t(q4, kv[:, :PART]) * SCALE, -1e30)
        o = pick_heads(dot(softmax(sc), kv), v_masks)
        pt[i] = dot(o, w_to[...]).astype(BF16).reshape(4, RUN, D)
        for k in (2, 1, 3):
            send(remote(pt.at[i, (x + k) % 4], r7.at[i, x], s7.at[i * 4 + k], d7.at[i * 4 + x], xdev(k)))

    def stage_second(n, u):
        i = n * CUT + u
        total = summed(pt[i, x], r7, i, d7)
        blk2[i, x] = (blk[i, x].astype(F32) + mod[5:6] * total).astype(BF16)
        gather(blk2, i, s7b, d7b)

    def stage_mlp(n, u):
        for v in range(CUT):
            others(blk2, n * CUT + v, d7b)
        normed = modulate(blk2[n * CUT : (n + 1) * CUT].reshape(128, D).astype(F32), mod[6:7], mod[7:8])
        hidden = jax.nn.gelu(dot(normed, w_up[...]), approximate=True).astype(BF16)
        out = dot(hidden, w_dp[...])
        for xd in range(4):
            rest = [out[32 * k : 32 * k + 32, 1024 + 32 * xd : 1056 + 32 * xd] for k in range(4)]
            pmp[n, xd] = jnp.concatenate(
                [out[:, 256 * xd : 256 * xd + 128], out[:, 256 * xd + 128 : 256 * xd + 256],
                 jnp.concatenate(rest, axis=1)], axis=0,
            ).astype(BF16)
            send_if(x != xd, remote(
                pmp.at[n, xd], r8.at[n, x], s8.at[n * 4 + xd], d8.at[n * 4 + x], dev(zlo, c, zhi, y, xd)
            ))

    def stage_return(n, u):
        lanes = pl.ds(pl.multiple_of(x * 256, 128), COVER)
        shift = (COVER - 32 * x) % COVER
        gate = pltpu.roll(jnp.broadcast_to(mod[8:9, lanes], (8, COVER)), shift, 1)[:1, :PART]
        base = pltpu.roll(blk2[n * CUT : (n + 1) * CUT, :, :, lanes].reshape(128, COVER).astype(F32), shift, 1)[:, :PART]
        total = unpack_part(summed(pmp[n, x], r8, n, d8))
        out = (base + gate * total).astype(BF16)
        fin[n] = dot(turn[...], out).astype(BF16).reshape(8, 16, PART)
        y_to = 2 * c + row_of[n]

        def back(j, kc):
            zd, cd = z_far[j], (c + kc) % 2
            return remote(
                fin.at[n, 2 * zd + cd], o_ref.at[m_me], s9.at[n * 8 + j * 2 + kc], d9.at[m_me], dev(zd, cd, zhi, y_to, x)
            )

        for j in range(4):
            for kc in range(2):
                if j < 3 or kc:
                    send(back(j, kc))
        here = y_to == y
        send_if(jnp.logical_not(here), back(3, 0))

        @pl.when(here)
        def _():
            pltpu.make_async_copy(fin.at[n, 2 * zlo + c], o_ref.at[m_me], d9.at[m_me]).start()

    for k in (3, 4):
        loads[k].wait()
    stages = (stage_spread, stage_gather, stage_temporal, stage_second, stage_mlp, stage_return)
    for k, n, u in ORDER:
        stages[k](n, u)
        if (k, n) == (1, 1):
            pl.semaphore_signal(csem, inc=1, device_id=dev(zlo, 1 - c, zhi, y, x), device_id_type=MESH)
        if (k, n) == (4, 0):
            pl.semaphore_wait(csem, 1)

    for done in sent:
        done()
    for m in range(16):
        arrived(o_ref.at[m], d9.at[m])


def body(latents, modulation, spatial_qkv, spatial_out, temporal_qkv, temporal_out, mlp_up, mlp_down):
    anywhere = pl.BlockSpec(memory_space=pl.ANY)
    sem = pltpu.SemaphoreType.DMA

    def vm(*shape):
        return pltpu.VMEM(shape, BF16)

    out = pl.pallas_call(
        kernel,
        out_shape=pltpu.VMEM((16, 16, PART), BF16),
        in_specs=[anywhere] * 8,
        out_specs=anywhere,
        scratch_shapes=[
            pltpu.VMEM((9, D), F32),
            vm(3 * PART, D), vm(PART, D), vm(3 * PART, D), vm(PART, D), vm(D, D), vm(D, D), vm(D, D),
            vm(D, 3 * PART), vm(D, 3 * PART),
            vm(2, 128, PART),
            vm(2, PART, 128),
            vm(4, 2, PART, 128),
            vm(2, 128, D),
            vm(2, 128, PART),
            vm(2, 128, 2 * PART),
            vm(2, 2 * PART, 128),
            vm(2, 2 * PART, 128),
            vm(2, 128, D),
            vm(2, 4, 32, D),
            vm(2, 32, D),
            vm(2, 16, 16, 256),
            vm(2, 16, 16, 256),
            vm(2 * CUT, 4, RUN, D),
            vm(2 * CUT, 4, RUN, D),
            vm(2 * CUT, 4, RUN, D),
            vm(2 * CUT, 4, RUN, D),
            vm(2, 4, PART, 128),
            vm(2, 4, PART, 128),
            vm(2, 8, 16, PART),
            vm(256, 160), vm(160, 256), vm(128, 128),
            sem((8,)),
            sem((8,)), sem((8,)), sem((2,)), sem((2,)), sem((8,)), sem((8,)), sem((32,)), sem((32,)),
            sem((8 * CUT,)), sem((8 * CUT,)), sem((8 * CUT,)), sem((8 * CUT,)), sem((8 * CUT,)), sem((8 * CUT,)),
            sem((8,)), sem((8,)), sem((16,)), sem((16,)),
            pltpu.SemaphoreType.REGULAR, pltpu.SemaphoreType.REGULAR, pltpu.SemaphoreType.REGULAR,
            pltpu.SemaphoreType.REGULAR, pltpu.SemaphoreType.REGULAR,
        ],
        compiler_params=pltpu.CompilerParams(
            collective_id=0, has_side_effects=True, vmem_limit_bytes=60 * 2**20
        ),
        name="block",
    )(
        latents.reshape(2, 128, PART), modulation,
        jnp.swapaxes(spatial_qkv, 1, 2).reshape(3 * PART, D), spatial_out,
        jnp.swapaxes(temporal_qkv, 1, 2).reshape(3 * PART, D), temporal_out, mlp_up, mlp_down,
    )
    return out.reshape(16, 2, 8, PART).transpose(1, 0, 2, 3).reshape(latents.shape)


def solution(mesh):
    return jax.shard_map(
        body,
        mesh=mesh,
        in_specs=(
            P("tm", "height", None, "head"),
            P(),
            P(None, None, "head"),
            P("head", None),
            P(None, None, "head"),
            P("head", None),
            P(None, "head"),
            P("head", None),
        ),
        out_specs=P("tm", "height", None, "head"),
        check_vma=False,
    )
```
